32 devices in a mesh: energy: 8 (over z, core), seg: 4 (over y, x).
Axes of the slice: x: 2, y: 2, z: 4, core: 2. Of those that a mesh axis runs over, the one named last changes fastest.
Arguments:
- green: bfloat16 [16, 4, 4, 128, 128], P('energy', 'seg'), may hold values from -6 to 6
- couple: bfloat16 [4, 4, 2, 128, 128], P('seg'), may hold values from -0.375 to 0.375
- phonon: float32 [4, 4, 3, 2], P('seg'), may hold values from 0.2 to 2
- neighbour: int32 [4, 4], P('seg'), may hold values from -1 to 1, as said below
- offsets: int32 [3], replicated, may hold values from 1 to 2, as said below
- counts: int32 [8], P('energy'), may hold values from 1 to 2, as said below
Outputs:
- sigma: float32 [16, 4, 4, 128, 128], P('energy', 'seg')
- polar: float32 [4, 768, 128], P('seg', 'energy')
The draws below stay inside these ranges and needn't reach their ends.
Inputs may be any that keep to these rules, and one draw needn't show every extreme that they name: `neighbour`: each segment's list holds -1, 0 and +1 in some order, the fourth entry also one of these. `offsets`: some offset equals 2. `counts`: some block has all 2 points live.
All inputs are finite; a program needn't handle non-finite values.
Results may differ from the reference program's by a relative error of at most 0.009.
Values may be sent and summed in bfloat16 or wider, within the bound.
A program may use at most 64 MiB of HBM per device.

```python
import math
import jax
import jax.numpy as jnp
from jax import lax

NB = 128
E_DEV = 2
NOFF = 3
NNBR = 4
NE = 16
NS = 4
ENERGY_BLOCKS = 8
N_ENERGY = 8


def draw_neighbour(key, part):
    first, second = jax.random.split(jax.random.fold_in(key, 11))
    extra = jax.random.randint(first, (NS,), -1, 2)
    base = jnp.broadcast_to(jnp.array([-1, 0, 1], jnp.int32), (NS, 3))
    rows = jnp.concatenate([base, extra[:, None].astype(jnp.int32)], axis=1)
    scores = jax.random.randint(second, (NS, 4), 0, 1 << 20) * 4 + jnp.arange(4, dtype=jnp.int32)[None, :]
    order = jnp.argsort(scores, axis=1)
    return jnp.take_along_axis(rows, order, axis=1).astype(jnp.int32)


def draw_offsets(key, part):
    first, second = jax.random.split(jax.random.fold_in(key, 12))
    values = jax.random.randint(first, (NOFF,), 1, E_DEV + 1)
    where = jax.random.randint(second, (), 0, NOFF)
    return jnp.where(jnp.arange(NOFF) == where, E_DEV, values).astype(jnp.int32)


def draw_counts(key, part):
    first, second = jax.random.split(jax.random.fold_in(key, 13))
    values = jax.random.randint(first, (ENERGY_BLOCKS,), (E_DEV + 1) // 2, E_DEV + 1)
    where = jax.random.randint(second, (), 0, ENERGY_BLOCKS)
    return jnp.where(jnp.arange(ENERGY_BLOCKS) == where, E_DEV, values).astype(jnp.int32)


def strengthened(result, rng, source, target, parts, factor):
    owner, partner = [(jnp.arange(result.shape[axis_at]) // (result.shape[axis_at] // parts)).reshape([-1 if axis == axis_at else 1 for axis in range(result.ndim)]) for axis_at in (source, target)]
    chosen = jax.random.permutation(rng, parts)[partner]
    strong = (owner == chosen) | (owner == (partner + parts // 2) % parts)
    return jnp.where(strong, factor * result, result)


def shard_levels(own_key, dims, pieces, low, largest):
    level = 1.0
    for axis_at, blocks in pieces:
        heights = jax.random.uniform(jax.random.fold_in(jax.random.fold_in(own_key, 6), axis_at), (blocks,), jnp.float32, low / len(pieces), largest / len(pieces))
        level = level * jnp.repeat(jnp.exp(heights), dims[axis_at] // blocks).reshape((-1,) + (1,) * (len(dims) - 1 - axis_at))
    return level


def gaussian(rng, extent, deviation, bound, cuts=(), kind=jnp.bfloat16):
    gain = shard_levels(rng, extent, cuts, -0.22, 0.18) if cuts else 1.0
    result = jax.random.normal(rng, extent, jnp.float32) * deviation * gain
    return jnp.minimum(jnp.maximum(result, -bound), bound).astype(kind)


def noise_with(key, extent, scale, most, pieces, heavy, kind=jnp.bfloat16):
    drawn = scale * jax.random.normal(key, extent, jnp.float32)
    if pieces:
        drawn = drawn * shard_levels(key, extent, pieces, -0.22, 0.18)
    return jnp.clip(strengthened(drawn, jax.random.fold_in(key, 3), *heavy), -most, most).astype(kind)


def setup_inputs(seed: int = 0) -> dict:
    streams_of = jax.random.split(jax.random.key(seed), 7)
    return {
        "green": noise_with(streams_of[0], (NE, NS, 4, NB, NB), 1.0, 6.0, ((0, 8), (1, 4)), (0, 3, 8, 2.0)),
        "couple": gaussian(streams_of[1], (NS, NNBR, 2, NB, NB), (2 * NB) ** -0.5, 0.375, ((0, 4),)),
        "phonon": jnp.clip(jnp.exp(math.log(2.0) - 2.3025851 * jax.random.uniform(streams_of[2], (NS, NNBR, NOFF, 2), jnp.float32) ** shard_levels(streams_of[2], (NS, NNBR, NOFF, 2), ((0, 4),), -0.2, 0.2)), 0.2, 2.0),
        "neighbour": draw_neighbour(jax.random.fold_in(streams_of[6], 71), 0),
        "offsets": draw_offsets(jax.random.fold_in(streams_of[6], 71), 0),
        "counts": draw_counts(jax.random.fold_in(streams_of[6], 71), 0),
    }


def local_terms(window, couple, phonon, neighbour, offsets, width):
    f32 = jnp.float32
    select = (neighbour[:, None] + 1 == jnp.arange(3, dtype=jnp.int32)[None, :]).astype(f32)
    size = window.shape[-1]
    lesser = jnp.zeros((width, 4, 2, size, size), f32)
    greater = jnp.zeros((width, 4, 2, size, size), f32)
    centre = window[width:2 * width, 1, 2:4].astype(f32)
    polar_rows = []
    for m in range(3):
        upper = lax.dynamic_slice_in_dim(window, width + offsets[m], width, 0).astype(f32)
        lower = lax.dynamic_slice_in_dim(window, width - offsets[m], width, 0).astype(f32)
        absorb = phonon[:, m, 0][:, None] * select
        emit = phonon[:, m, 1][:, None] * select
        lesser = lesser + jnp.einsum('nc,ecpij->enpij', absorb, upper[:, :, 0:2]) + jnp.einsum('nc,ecpij->enpij', emit, lower[:, :, 0:2])
        greater = greater + jnp.einsum('nc,ecpij->enpij', absorb, lower[:, :, 2:4]) + jnp.einsum('nc,ecpij->enpij', emit, upper[:, :, 2:4])
        own = upper[:, 1, 0:2]
        real_part = jnp.einsum('eij,ekj->ik', own[:, 0], centre[:, 0]) + jnp.einsum('eij,ekj->ik', own[:, 1], centre[:, 1])
        imag_part = jnp.einsum('eij,ekj->ik', own[:, 1], centre[:, 0]) - jnp.einsum('eij,ekj->ik', own[:, 0], centre[:, 1])
        polar_rows.append(real_part)
        polar_rows.append(imag_part)
    mixed = jnp.stack([lesser, greater], axis=2).astype(jnp.bfloat16).astype(f32)
    coup = couple.astype(f32)
    coup_re = coup[:, 0]
    coup_im = coup[:, 1]
    left_re = jnp.einsum('nij,enkjl->enkil', coup_re, mixed[:, :, :, 0]) - jnp.einsum('nij,enkjl->enkil', coup_im, mixed[:, :, :, 1])
    left_im = jnp.einsum('nij,enkjl->enkil', coup_re, mixed[:, :, :, 1]) + jnp.einsum('nij,enkjl->enkil', coup_im, mixed[:, :, :, 0])
    left_re = left_re.astype(jnp.bfloat16).astype(f32)
    left_im = left_im.astype(jnp.bfloat16).astype(f32)
    out_re = jnp.einsum('enkil,nml->ekim', left_re, coup_re) + jnp.einsum('enkil,nml->ekim', left_im, coup_im)
    out_im = jnp.einsum('enkil,nml->ekim', left_im, coup_re) - jnp.einsum('enkil,nml->ekim', left_re, coup_im)
    sigma = jnp.stack([out_re, out_im], axis=2).reshape(width, 4, size, size)
    polar = jnp.concatenate(polar_rows, axis=0)
    return sigma, polar


def reference(green, couple, phonon, neighbour, offsets, counts):
    position = jnp.arange(NE, dtype=jnp.int32)
    live = (position % E_DEV < jnp.repeat(counts, E_DEV, total_repeat_length=NE)).astype(jnp.bfloat16)
    masked = green * live[:, None, None, None, None]
    padded = jnp.pad(masked, ((E_DEV, E_DEV), (1, 1), (0, 0), (0, 0), (0, 0)))
    zero = jnp.zeros((), jnp.int32)

    def single(index):
        block = (index // NS).astype(jnp.int32)
        segment = (index % NS).astype(jnp.int32)
        window = lax.dynamic_slice(padded, (block * E_DEV, segment, zero, zero, zero), (3 * E_DEV, 3, 4, NB, NB))
        return local_terms(window, couple[segment], phonon[segment], neighbour[segment], offsets, E_DEV)

    sig, pol = lax.map(single, jnp.arange(N_ENERGY * NS, dtype=jnp.int32))
    sig = sig.reshape(N_ENERGY, NS, E_DEV, 4, NB, NB).transpose(0, 2, 1, 3, 4, 5).reshape(NE, NS, 4, NB, NB)
    pol = jnp.sum(pol.reshape(N_ENERGY, NS, 6 * NB, NB), axis=0)
    return sig, pol
```

```python
import functools

import jax
import jax.numpy as jnp
from jax import lax
from jax.experimental import pallas as pl
from jax.experimental.pallas import tpu as pltpu
from jax.sharding import PartitionSpec as P

F32 = jnp.float32
BF16 = jnp.bfloat16
NT = (((1,), (1,)), ((), ()))
NN = (((1,), (0,)), ((), ()))


def kernel(
    ne,
    ns,
    phonon,
    neighbour,
    offsets,
    counts,
    green,
    couple,
    sigma,
    polar,
    win,
    mixed,
    left,
    coup_a,
    coup_b,
    pol,
    slabs,
    pair_tx,
    pair_rx,
    part_tx,
    part_rx,
    e_send,
    e_recv,
    s_send,
    s_recv,
    pair_sem,
    part_send,
    part_recv,
):
    width, size = green.shape[0], green.shape[-1]
    nbr, noff = phonon.shape[1], phonon.shape[2]
    rows = polar.shape[1]
    half = ne // 2
    me, seg = lax.axis_index("energy"), lax.axis_index("seg")
    core, chip = lax.rem(me, 2), lax.div(me, 2)
    sibling = me + 1 - 2 * core
    has_next, has_prev = me < ne - 1, me > 0
    has_right, has_left = seg < ns - 1, seg > 0

    def e_copy(way, slot, j):
        there = jnp.minimum(me + 1, ne - 1) if way == 0 else jnp.maximum(me - 1, 0)
        return pltpu.make_async_remote_copy(
            src_ref=win.at[slot, width + j],
            dst_ref=win.at[slot, 2 * width * way + j],
            send_sem=e_send.at[way, slot, j],
            recv_sem=e_recv.at[way, slot, j],
            device_id={"energy": there},
            device_id_type=pl.DeviceIdType.MESH,
        )

    def s_copy(way, j):
        there = jnp.minimum(seg + 1, ns - 1) if way == 0 else jnp.maximum(seg - 1, 0)
        return pltpu.make_async_remote_copy(
            src_ref=win.at[1, width + j],
            dst_ref=win.at[2 * way, width + j],
            send_sem=s_send.at[way, j],
            recv_sem=s_recv.at[way, j],
            device_id={"seg": there},
            device_id_type=pl.DeviceIdType.MESH,
        )

    e_out, e_in = (has_next, has_prev), (has_prev, has_next)
    s_out, s_in = (has_right, has_left), (has_left, has_right)

    barrier = pltpu.get_barrier_semaphore()

    def greet(cond, where):
        @pl.when(cond)
        def _():
            pl.semaphore_signal(
                barrier, inc=1, device_id=where, device_id_type=pl.DeviceIdType.MESH
            )

    greet(has_next, {"energy": jnp.minimum(me + 1, ne - 1)})
    greet(has_prev, {"energy": jnp.maximum(me - 1, 0)})
    greet(has_right, {"seg": jnp.minimum(seg + 1, ns - 1)})
    greet(has_left, {"seg": jnp.maximum(seg - 1, 0)})

    def greet_part(k, carry):
        there = lax.rem(chip + k, half) * 2 + core
        pl.semaphore_signal(
            barrier,
            inc=1,
            device_id={"energy": there},
            device_id_type=pl.DeviceIdType.MESH,
        )
        return carry

    lax.fori_loop(1, half, greet_part, 0)

    for e in range(width):
        own = green[e, 0]
        win[1, width + e] = jnp.where(e < counts[0], own, jnp.zeros_like(own))

    @pl.when(jnp.logical_not(has_prev))
    def _():
        win[:, :width] = jnp.zeros((3, width) + win.shape[2:], BF16)

    @pl.when(jnp.logical_not(has_next))
    def _():
        win[:, 2 * width :] = jnp.zeros((3, width) + win.shape[2:], BF16)

    for slot, cond in ((0, has_left), (2, has_right)):

        @pl.when(jnp.logical_not(cond))
        def _():
            win[slot] = jnp.zeros(win.shape[1:], BF16)

    total = (
        has_next.astype(jnp.int32)
        + has_prev.astype(jnp.int32)
        + has_right.astype(jnp.int32)
        + has_left.astype(jnp.int32)
        + (half - 1)
    )
    pl.semaphore_wait(barrier, total)

    for j in range(width):
        for way in range(2):
            pl.when(s_out[way])(lambda: s_copy(way, j).start())
        for way in range(2):
            pl.when(e_out[way])(lambda: e_copy(way, 1, j).start())

    for n in range(nbr):
        re, im = couple[0, n, 0], couple[0, n, 1]
        coup_a[n, :size, :size] = re
        coup_a[n, :size, size:] = -im
        coup_a[n, size:, :size] = im
        coup_a[n, size:, size:] = re
        at = 2 * n * size
        coup_b[:size, at : at + size] = re
        coup_b[:size, at + size : at + 2 * size] = im
        coup_b[size:, at : at + size] = -im
        coup_b[size:, at + size : at + 2 * size] = re

    for j in range(width):
        for way in range(2):
            slot = 2 * way

            @pl.when(s_in[way])
            def _():
                s_copy(way, j).wait_recv()
                for to in range(2):
                    pl.when(e_out[to])(lambda: e_copy(to, slot, j).start())

    for j in range(width):
        pl.when(e_in[1])(lambda: e_copy(1, 1, j).wait_recv())

    def pair(ref, e, p):
        return jnp.concatenate([ref[1, e, p], ref[1, e, p + 1]], axis=1)

    total = None
    for e in range(width):
        lower = jnp.concatenate(
            [pair(win, width + e + d, 0) for d in range(1, width + 1)], axis=0
        )
        re, im = win[1, width + e, 2], win[1, width + e, 3]
        upper = jnp.concatenate(
            [
                jnp.concatenate([re, im], axis=1),
                jnp.concatenate([-im, re], axis=1),
            ],
            axis=0,
        )
        term = lax.dot_general(lower, upper, NT, preferred_element_type=F32)
        total = term if total is None else total + term
    for m in range(noff):
        chosen = total[:size]
        for d in range(2, width + 1):
            chosen = jnp.where(
                offsets[m] == d, total[(d - 1) * size : d * size], chosen
            )
        pol[2 * m * size : (2 * m + 1) * size] = chosen[:, :size]
        pol[(2 * m + 1) * size : (2 * m + 2) * size] = chosen[:, size:]
    padded = slabs.shape[1]
    for d in range(ne):
        if padded > rows:
            slabs[d, rows:] = jnp.zeros((padded - rows, size), F32)
        slabs[d, :rows] = pol[d * rows : (d + 1) * rows]

    def fill(q, carry):
        pair_tx[q] = slabs[2 * q + 1 - core].astype(BF16)
        return carry

    lax.fori_loop(0, half, fill, 0)
    to_sibling = pltpu.make_async_remote_copy(
        src_ref=pair_tx,
        dst_ref=pair_rx,
        send_sem=pair_sem.at[0],
        recv_sem=pair_sem.at[1],
        device_id={"energy": sibling},
        device_id_type=pl.DeviceIdType.MESH,
    )
    to_sibling.start()
    to_sibling.wait_recv()

    def part_copy(k):
        there = lax.rem(chip + k, half)
        return pltpu.make_async_remote_copy(
            src_ref=part_tx.at[there],
            dst_ref=part_rx.at[chip],
            send_sem=part_send.at[k],
            recv_sem=part_recv.at[k],
            device_id={"energy": there * 2 + core},
            device_id_type=pl.DeviceIdType.MESH,
        )

    def send_part(k, carry):
        there = lax.rem(chip + k, half)
        value = slabs[2 * there + core] + pair_rx[there].astype(F32)
        part_tx[there] = value.astype(BF16)
        part_copy(k).start()
        return carry

    lax.fori_loop(1, half, send_part, 0)

    for slot in range(3):
        for way in range(2):
            for j in range(width):
                if (slot, way) == (1, 1):
                    continue
                cond = e_in[way]
                if slot != 1:
                    cond = jnp.logical_and(cond, s_in[slot // 2])
                pl.when(cond)(lambda: e_copy(way, slot, j).wait_recv())

    weights = []
    for n in range(nbr):
        up, down = [None], [None]
        for d in range(1, width + 1):
            a = b = jnp.float32(0)
            for m in range(noff):
                hit = offsets[m] == d
                a = a + jnp.where(hit, phonon[0, n, m, 0], 0.0)
                b = b + jnp.where(hit, phonon[0, n, m, 1], 0.0)
            up.append(a)
            down.append(b)
        weights.append((up, down))

    chunk = 16
    for p in range(4):
        k, ri = p // 2, p % 2

        def mix(t, carry, p=p, k=k, ri=ri):
            r = pl.multiple_of(t * chunk, chunk)
            g = [
                [win[c, e, p, pl.ds(r, chunk), :] for e in range(3 * width)]
                for c in range(3)
            ]
            for n in range(nbr):
                to = neighbour[0, n]
                chosen = [
                    jnp.where(
                        to == 0, g[1][e], jnp.where(to < 0, g[0][e], g[2][e])
                    ).astype(F32)
                    for e in range(3 * width)
                ]
                up, down = weights[n] if k == 0 else weights[n][::-1]
                for e in range(width):
                    acc = None
                    for d in range(1, width + 1):
                        term = (
                            up[d] * chosen[width + e + d]
                            + down[d] * chosen[width + e - d]
                        )
                        acc = term if acc is None else acc + term
                    at = (2 * e + k) * size
                    mixed[n, pl.ds(ri * size + r, chunk), at : at + size] = acc.astype(
                        BF16
                    )
            return carry

        lax.fori_loop(0, size // chunk, mix, 0)

    for n in range(nbr):
        y = lax.dot_general(
            coup_a[n], mixed[n], NN, preferred_element_type=F32
        ).astype(BF16)
        for ek in range(2 * width):
            for ri in range(2):
                at = (2 * n + ri) * size
                left[ek * size : (ek + 1) * size, at : at + size] = y[
                    ri * size : (ri + 1) * size, ek * size : (ek + 1) * size
                ]
    for ek in range(2 * width):
        out = lax.dot_general(
            left[ek * size : (ek + 1) * size],
            coup_b[...],
            NT,
            preferred_element_type=F32,
        )
        e, k = ek // 2, ek % 2
        sigma[e, 0, 2 * k] = out[:, :size]
        sigma[e, 0, 2 * k + 1] = out[:, size:]

    def wait_part(k, carry):
        part_copy(k).wait()
        return carry

    lax.fori_loop(1, half, wait_part, 0)
    mine = slabs[me] + pair_rx[chip].astype(F32)

    def add_part(k, acc):
        return acc + part_rx[lax.rem(chip + k, half)].astype(F32)

    mine = lax.fori_loop(1, half, add_part, mine)
    polar[0] = mine[:rows]

    to_sibling.wait_send()
    for j in range(width):
        for way in range(2):
            pl.when(s_out[way])(lambda: s_copy(way, j).wait_send())
            for slot in range(3):
                cond = e_out[way]
                if slot != 1:
                    cond = jnp.logical_and(cond, s_in[slot // 2])
                pl.when(cond)(lambda: e_copy(way, slot, j).wait_send())


def local(ne, ns, green, couple, phonon, neighbour, offsets, counts):
    width, size = green.shape[0], green.shape[-1]
    nbr, noff = phonon.shape[1], phonon.shape[2]
    rows = 2 * noff * size // ne
    padded = -(-rows // 16) * 16
    half = ne // 2
    smem = pl.BlockSpec(memory_space=pltpu.SMEM)
    vmem = pl.BlockSpec(memory_space=pltpu.VMEM)
    dma = pltpu.SemaphoreType.DMA
    return pl.pallas_call(
        functools.partial(kernel, ne, ns),
        out_shape=(
            jax.ShapeDtypeStruct(green.shape, F32),
            jax.ShapeDtypeStruct((1, rows, size), F32),
        ),
        in_specs=[smem] * 4 + [vmem] * 2,
        out_specs=(vmem, vmem),
        scratch_shapes=[
            pltpu.VMEM((3, 3 * width, 4, size, size), BF16),
            pltpu.VMEM((nbr, 2 * size, 2 * width * size), BF16),
            pltpu.VMEM((2 * width * size, 2 * nbr * size), BF16),
            pltpu.VMEM((nbr, 2 * size, 2 * size), BF16),
            pltpu.VMEM((2 * size, 2 * nbr * size), BF16),
            pltpu.VMEM((2 * noff * size, size), F32),
            pltpu.VMEM((ne, padded, size), F32),
            pltpu.VMEM((half, padded, size), BF16),
            pltpu.VMEM((half, padded, size), BF16),
            pltpu.VMEM((half, padded, size), BF16),
            pltpu.VMEM((half, padded, size), BF16),
            dma((2, 3, width)),
            dma((2, 3, width)),
            dma((2, width)),
            dma((2, width)),
            dma((2,)),
            dma((half,)),
            dma((half,)),
        ],
        compiler_params=pltpu.CompilerParams(
            collective_id=0, has_side_effects=True, vmem_limit_bytes=32 * 1024 * 1024
        ),
        cost_estimate=pl.CostEstimate(
            flops=600_000_000, bytes_accessed=4_000_000, transcendentals=0
        ),
    )(phonon, neighbour, offsets, counts, green, couple)


def solution(mesh):
    placed = (
        P("energy", "seg", None, None, None),
        P("seg", None, None, None, None),
        P("seg", None, None, None),
        P("seg", None),
        P(),
        P("energy"),
    )
    return jax.shard_map(
        functools.partial(local, mesh.shape["energy"], mesh.shape["seg"]),
        mesh=mesh,
        in_specs=placed,
        out_specs=(P("energy", "seg", None, None, None), P("seg", "energy", None)),
        check_vma=False,
    )
```

```python
import functools

import jax
import jax.numpy as jnp
from jax import lax
from jax.experimental import pallas as pl
from jax.experimental.pallas import tpu as pltpu
from jax.sharding import PartitionSpec as P

F32 = jnp.float32
BF16 = jnp.bfloat16
NT = (((1,), (1,)), ((), ()))
NN = (((1,), (0,)), ((), ()))


def kernel(
    ne,
    ns,
    phonon,
    neighbour,
    offsets,
    counts,
    green,
    couple,
    sigma,
    polar,
    raw,
    coup,
    win,
    mixed,
    left,
    coup_a,
    coup_b,
    pol,
    slabs,
    pair_tx,
    pair_rx,
    part_tx,
    part_rx,
    load_sem,
    e_send,
    e_recv,
    s_send,
    s_recv,
    pair_sem,
    part_send,
    part_recv,
):
    width, size = green.shape[0], green.shape[-1]
    nbr, noff = couple.shape[1], phonon.shape[1]
    rows = polar.shape[1]
    half = ne // 2
    me, seg = lax.axis_index("energy"), lax.axis_index("seg")
    core, chip = lax.rem(me, 2), lax.div(me, 2)
    sibling = me + 1 - 2 * core
    side = lax.rem(seg, 2)
    has_next, has_prev = me < ne - 1, me > 0
    partner = seg + 1 - 2 * side
    above, below = seg + 2 < ns, seg >= 2
    even = side == 0
    far_out = jnp.logical_or(
        jnp.logical_and(even, above), jnp.logical_and(jnp.logical_not(even), below)
    )
    far_in = jnp.logical_or(
        jnp.logical_and(even, below), jnp.logical_and(jnp.logical_not(even), above)
    )
    far_to = jnp.clip(seg + 2 - 4 * side, 0, ns - 1)
    far_from = jnp.clip(seg - 2 + 4 * side, 0, ns - 1)
    near, far = 2 - 2 * side, 2 * side
    slots = (1, near, far)
    mesh_type = pl.DeviceIdType.MESH
    chunks = [(k, j) for k in range(2) for j in range(width)]

    loads = [
        pltpu.make_async_copy(green.at[:, 0], raw, load_sem.at[0]),
        pltpu.make_async_copy(couple.at[0], coup, load_sem.at[1]),
    ]

    def e_copy(way, kind, k, j):
        there = jnp.minimum(me + 1, ne - 1) if way == 0 else jnp.maximum(me - 1, 0)
        return pltpu.make_async_remote_copy(
            src_ref=win.at[slots[kind], width + j, pl.ds(2 * k, 2)],
            dst_ref=win.at[slots[kind], 2 * width * way + j, pl.ds(2 * k, 2)],
            send_sem=e_send.at[way, kind, k, j],
            recv_sem=e_recv.at[way, kind, k, j],
            device_id={"energy": there},
            device_id_type=mesh_type,
        )

    def s_copy(kind, k, j):
        return pltpu.make_async_remote_copy(
            src_ref=win.at[1 if kind == 0 else near, width + j, pl.ds(2 * k, 2)],
            dst_ref=win.at[far, width + j, pl.ds(2 * k, 2)],
            send_sem=s_send.at[kind, k, j],
            recv_sem=s_recv.at[kind, k, j],
            device_id={"seg": partner if kind == 0 else far_to},
            device_id_type=mesh_type,
        )

    e_out, e_in = (has_next, has_prev), (has_prev, has_next)

    barrier = pltpu.get_barrier_semaphore()

    def greet(where):
        pl.semaphore_signal(barrier, inc=1, device_id=where, device_id_type=mesh_type)

    pl.when(has_next)(lambda: greet({"energy": jnp.minimum(me + 1, ne - 1)}))
    pl.when(has_prev)(lambda: greet({"energy": jnp.maximum(me - 1, 0)}))
    greet({"seg": partner})
    pl.when(far_out)(lambda: greet({"seg": far_to}))
    pl.when(far_in)(lambda: greet({"seg": far_from}))

    def greet_part(k, carry):
        greet({"energy": lax.rem(chip + k, half) * 2 + core})
        return carry

    lax.fori_loop(1, half, greet_part, 0)
    for load in loads:
        load.start()

    @pl.when(jnp.logical_not(has_prev))
    def _():
        win[:, :width] = jnp.zeros((3, width) + win.shape[2:], BF16)

    @pl.when(jnp.logical_not(has_next))
    def _():
        win[:, 2 * width :] = jnp.zeros((3, width) + win.shape[2:], BF16)

    @pl.when(jnp.logical_not(far_in))
    def _():
        win[far] = jnp.zeros(win.shape[1:], BF16)

    loads[0].wait()
    for e in range(width):
        own = raw[e]
        win[1, width + e] = jnp.where(e < counts[0], own, jnp.zeros_like(own))

    total = 1 + half - 1
    for cond in (has_next, has_prev, far_out, far_in):
        total = total + cond.astype(jnp.int32)
    pl.semaphore_wait(barrier, total)

    for k, j in chunks:
        s_copy(0, k, j).start()
        for way in range(2):
            pl.when(e_out[way])(lambda: e_copy(way, 0, k, j).start())

    loads[1].wait()
    for n in range(nbr):
        re, im = coup[n, 0], coup[n, 1]
        coup_a[n, :size, :size] = re
        coup_a[n, :size, size:] = -im
        coup_a[n, size:, :size] = im
        coup_a[n, size:, size:] = re
        at = 2 * n * size
        coup_b[:size, at : at + size] = re
        coup_b[:size, at + size : at + 2 * size] = im
        coup_b[size:, at : at + size] = -im
        coup_b[size:, at + size : at + 2 * size] = re

    def pass_near(k, j):
        s_copy(0, k, j).wait_recv()
        pl.when(far_out)(lambda: s_copy(1, k, j).start())
        for way in range(2):
            pl.when(e_out[way])(lambda: e_copy(way, 1, k, j).start())

    def pass_far(k, j):
        @pl.when(far_in)
        def _():
            s_copy(1, k, j).wait_recv()
            for way in range(2):
                pl.when(e_out[way])(lambda: e_copy(way, 2, k, j).start())

    def pair(e, p):
        return jnp.concatenate([win[1, e, p], win[1, e, p + 1]], axis=1)

    to_sibling = pltpu.make_async_remote_copy(
        src_ref=pair_tx,
        dst_ref=pair_rx,
        send_sem=pair_sem.at[0],
        recv_sem=pair_sem.at[1],
        device_id={"energy": sibling},
        device_id_type=mesh_type,
    )

    def own_polar():
        total = None
        for e in range(width):
            lower = jnp.concatenate(
                [pair(width + e + d, 0) for d in range(1, width + 1)], axis=0
            )
            re, im = win[1, width + e, 2], win[1, width + e, 3]
            upper = jnp.concatenate(
                [
                    jnp.concatenate([re, im], axis=1),
                    jnp.concatenate([-im, re], axis=1),
                ],
                axis=0,
            )
            term = lax.dot_general(lower, upper, NT, preferred_element_type=F32)
            total = term if total is None else total + term
        for m in range(noff):
            chosen = total[:size]
            for d in range(2, width + 1):
                chosen = jnp.where(
                    offsets[m] == d, total[(d - 1) * size : d * size], chosen
                )
            pol[2 * m * size : (2 * m + 1) * size] = chosen[:, :size]
            pol[(2 * m + 1) * size : (2 * m + 2) * size] = chosen[:, size:]
        padded = slabs.shape[1]
        for d in range(ne):
            if padded > rows:
                slabs[d, rows:] = jnp.zeros((padded - rows, size), F32)
            slabs[d, :rows] = pol[d * rows : (d + 1) * rows]

        def fill(q, carry):
            pair_tx[q] = slabs[2 * q + 1 - core].astype(BF16)
            return carry

        lax.fori_loop(0, half, fill, 0)
        to_sibling.start()

    def part_copy(k):
        there = lax.rem(chip + k, half)
        return pltpu.make_async_remote_copy(
            src_ref=part_tx.at[there],
            dst_ref=part_rx.at[chip],
            send_sem=part_send.at[k],
            recv_sem=part_recv.at[k],
            device_id={"energy": there * 2 + core},
            device_id_type=mesh_type,
        )

    def send_part(k, carry):
        there = lax.rem(chip + k, half)
        value = slabs[2 * there + core] + pair_rx[there].astype(F32)
        part_tx[there] = value.astype(BF16)
        part_copy(k).start()
        return carry

    pass_near(*chunks[0])
    for j in range(width):
        pl.when(e_in[1])(lambda: e_copy(1, 0, 0, j).wait_recv())
    own_polar()
    for i in range(1, len(chunks)):
        pass_near(*chunks[i])
        pass_far(*chunks[i - 1])
    pass_far(*chunks[-1])
    to_sibling.wait_recv()
    lax.fori_loop(1, half, send_part, 0)

    weights = []
    for n in range(nbr):
        up, down = [None], [None]
        for d in range(1, width + 1):
            a = b = jnp.float32(0)
            for m in range(noff):
                hit = offsets[m] == d
                a = a + jnp.where(hit, phonon[0, m, 0, n], 0.0)
                b = b + jnp.where(hit, phonon[0, m, 1, n], 0.0)
            up.append(a)
            down.append(b)
        weights.append((up, down))

    tile = 16
    for k in range(2):
        for kind in range(3):
            for way in range(2):
                for j in range(width):
                    if (kind, way, k) == (0, 1, 0):
                        continue
                    cond = e_in[way]
                    if kind == 2:
                        cond = jnp.logical_and(cond, far_in)
                    pl.when(cond)(lambda: e_copy(way, kind, k, j).wait_recv())

        for ri in range(2):
            p = 2 * k + ri

            def mix(t, carry, p=p, k=k, ri=ri):
                r = pl.multiple_of(t * tile, tile)
                g = [
                    [win[c, e, p, pl.ds(r, tile), :] for e in range(3 * width)]
                    for c in range(3)
                ]
                for n in range(nbr):
                    to = neighbour[0, n]
                    chosen = [
                        jnp.where(
                            to == 0, g[1][e], jnp.where(to < 0, g[0][e], g[2][e])
                        ).astype(F32)
                        for e in range(3 * width)
                    ]
                    up, down = weights[n] if k == 0 else weights[n][::-1]
                    for e in range(width):
                        acc = None
                        for d in range(1, width + 1):
                            term = (
                                up[d] * chosen[width + e + d]
                                + down[d] * chosen[width + e - d]
                            )
                            acc = term if acc is None else acc + term
                        at = (k * width + e) * size
                        mixed[n, pl.ds(ri * size + r, tile), at : at + size] = (
                            acc.astype(BF16)
                        )
                return carry

            lax.fori_loop(0, size // tile, mix, 0)

        first = k * width * size
        for n in range(nbr):
            y = lax.dot_general(
                coup_a[n],
                mixed[n, :, first : first + width * size],
                NN,
                preferred_element_type=F32,
            ).astype(BF16)
            for e in range(width):
                for ri in range(2):
                    at = (2 * n + ri) * size
                    left[first + e * size : first + (e + 1) * size, at : at + size] = y[
                        ri * size : (ri + 1) * size, e * size : (e + 1) * size
                    ]
        for e in range(width):
            out = lax.dot_general(
                left[first + e * size : first + (e + 1) * size],
                coup_b[...],
                NT,
                preferred_element_type=F32,
            )
            sigma[e, 0, 2 * k] = out[:, :size]
            sigma[e, 0, 2 * k + 1] = out[:, size:]

    def wait_part(k, carry):
        part_copy(k).wait()
        return carry

    lax.fori_loop(1, half, wait_part, 0)
    mine = slabs[me] + pair_rx[chip].astype(F32)

    def add_part(k, acc):
        return acc + part_rx[lax.rem(chip + k, half)].astype(F32)

    mine = lax.fori_loop(1, half, add_part, mine)
    polar[0] = mine[:rows]

    to_sibling.wait_send()
    for k, j in chunks:
        s_copy(0, k, j).wait_send()
        pl.when(far_out)(lambda: s_copy(1, k, j).wait_send())
        for way in range(2):
            for kind in range(3):
                cond = e_out[way]
                if kind == 2:
                    cond = jnp.logical_and(cond, far_in)
                pl.when(cond)(lambda: e_copy(way, kind, k, j).wait_send())


def local(ne, ns, green, couple, phonon, neighbour, offsets, counts):
    width, size = green.shape[0], green.shape[-1]
    nbr, noff = couple.shape[1], phonon.shape[2]
    rows = 2 * noff * size // ne
    padded = -(-rows // 16) * 16
    half = ne // 2
    smem = pl.BlockSpec(memory_space=pltpu.SMEM)
    vmem = pl.BlockSpec(memory_space=pltpu.VMEM)
    dma = pltpu.SemaphoreType.DMA
    return pl.pallas_call(
        functools.partial(kernel, ne, ns),
        out_shape=(
            jax.ShapeDtypeStruct(green.shape, F32),
            jax.ShapeDtypeStruct((1, rows, size), F32),
        ),
        in_specs=[smem] * 4 + [pl.BlockSpec(memory_space=pltpu.HBM)] * 2,
        out_specs=(vmem, vmem),
        scratch_shapes=[
            pltpu.VMEM((width, 4, size, size), BF16),
            pltpu.VMEM((nbr, 2, size, size), BF16),
            pltpu.VMEM((3, 3 * width, 4, size, size), BF16),
            pltpu.VMEM((nbr, 2 * size, 2 * width * size), BF16),
            pltpu.VMEM((2 * width * size, 2 * nbr * size), BF16),
            pltpu.VMEM((nbr, 2 * size, 2 * size), BF16),
            pltpu.VMEM((2 * size, 2 * nbr * size), BF16),
            pltpu.VMEM((2 * noff * size, size), F32),
            pltpu.VMEM((ne, padded, size), F32),
            pltpu.VMEM((half, padded, size), BF16),
            pltpu.VMEM((half, padded, size), BF16),
            pltpu.VMEM((half, padded, size), BF16),
            pltpu.VMEM((half, padded, size), BF16),
            dma((2,)),
            dma((2, 3, 2, width)),
            dma((2, 3, 2, width)),
            dma((2, 2, width)),
            dma((2, 2, width)),
            dma((2,)),
            dma((half,)),
            dma((half,)),
        ],
        compiler_params=pltpu.CompilerParams(
            collective_id=0, has_side_effects=True, vmem_limit_bytes=32 * 1024 * 1024
        ),
        cost_estimate=pl.CostEstimate(
            flops=600_000_000, bytes_accessed=4_000_000, transcendentals=0
        ),
    )(jnp.transpose(phonon, (0, 2, 3, 1)), neighbour, offsets, counts, green, couple)


def solution(mesh):
    placed = (
        P("energy", "seg", None, None, None),
        P("seg", None, None, None, None),
        P("seg", None, None, None),
        P("seg", None),
        P(),
        P("energy"),
    )
    return jax.shard_map(
        functools.partial(local, mesh.shape["energy"], mesh.shape["seg"]),
        mesh=mesh,
        in_specs=placed,
        out_specs=(P("energy", "seg", None, None, None), P("seg", "energy", None)),
        check_vma=False,
    )
```

```python
import functools

import jax
import jax.numpy as jnp
from jax import lax
from jax.experimental import pallas as pl
from jax.experimental.pallas import tpu as pltpu
from jax.sharding import PartitionSpec as P

F32 = jnp.float32
BF16 = jnp.bfloat16
NT = (((1,), (1,)), ((), ()))
NN = (((1,), (0,)), ((), ()))


def kernel(
    ne,
    ns,
    phonon_in,
    neighbour_in,
    offsets_in,
    counts_in,
    green,
    couple,
    sigma_out,
    polar_out,
    phonon,
    neighbour,
    offsets,
    counts,
    sigma,
    polar,
    raw,
    coup,
    win,
    mixed,
    left,
    coup_a,
    coup_b,
    pol,
    slabs,
    pair_tx,
    pair_rx,
    part_tx,
    part_rx,
    load_sem,
    e_send,
    e_recv,
    s_send,
    s_recv,
    pair_sem,
    part_send,
    part_recv,
    out_sem,
):
    width, size = green.shape[0], green.shape[-1]
    nbr, noff = couple.shape[1], phonon_in.shape[1]
    rows = polar.shape[1]
    half = ne // 2
    me, seg = lax.axis_index("energy"), lax.axis_index("seg")
    core, chip = lax.rem(me, 2), lax.div(me, 2)
    sibling = me + 1 - 2 * core
    side = lax.rem(seg, 2)
    has_next, has_prev = me < ne - 1, me > 0
    partner = seg + 1 - 2 * side
    above, below = seg + 2 < ns, seg >= 2
    even = side == 0
    far_out = jnp.logical_or(
        jnp.logical_and(even, above), jnp.logical_and(jnp.logical_not(even), below)
    )
    far_in = jnp.logical_or(
        jnp.logical_and(even, below), jnp.logical_and(jnp.logical_not(even), above)
    )
    far_to = jnp.clip(seg + 2 - 4 * side, 0, ns - 1)
    far_from = jnp.clip(seg - 2 + 4 * side, 0, ns - 1)
    near, far = 2 - 2 * side, 2 * side
    slots = (1, near, far)
    mesh_type = pl.DeviceIdType.MESH
    chunks = [(k, j) for k in range(2) for j in range(width)]

    loads = [
        pltpu.make_async_copy(green.at[:, 0], raw, load_sem.at[0]),
        pltpu.make_async_copy(couple.at[0], coup, load_sem.at[1]),
        pltpu.make_async_copy(phonon_in, phonon, load_sem.at[2]),
        pltpu.make_async_copy(neighbour_in, neighbour, load_sem.at[3]),
        pltpu.make_async_copy(offsets_in, offsets, load_sem.at[4]),
        pltpu.make_async_copy(counts_in, counts, load_sem.at[5]),
    ]
    stores = [
        pltpu.make_async_copy(
            sigma.at[:, :, pl.ds(2 * k, 2)],
            sigma_out.at[:, :, pl.ds(2 * k, 2)],
            out_sem.at[k],
        )
        for k in range(2)
    ]
    stores.append(pltpu.make_async_copy(polar, polar_out, out_sem.at[2]))

    def e_copy(way, kind, k, j):
        there = jnp.minimum(me + 1, ne - 1) if way == 0 else jnp.maximum(me - 1, 0)
        return pltpu.make_async_remote_copy(
            src_ref=win.at[slots[kind], width + j, pl.ds(2 * k, 2)],
            dst_ref=win.at[slots[kind], 2 * width * way + j, pl.ds(2 * k, 2)],
            send_sem=e_send.at[way, kind, k, j],
            recv_sem=e_recv.at[way, kind, k, j],
            device_id={"energy": there},
            device_id_type=mesh_type,
        )

    def s_copy(kind, k, j):
        return pltpu.make_async_remote_copy(
            src_ref=win.at[1 if kind == 0 else near, width + j, pl.ds(2 * k, 2)],
            dst_ref=win.at[far, width + j, pl.ds(2 * k, 2)],
            send_sem=s_send.at[kind, k, j],
            recv_sem=s_recv.at[kind, k, j],
            device_id={"seg": partner if kind == 0 else far_to},
            device_id_type=mesh_type,
        )

    e_out, e_in = (has_next, has_prev), (has_prev, has_next)

    barrier = pltpu.get_barrier_semaphore()

    def greet(where):
        pl.semaphore_signal(barrier, inc=1, device_id=where, device_id_type=mesh_type)

    pl.when(has_next)(lambda: greet({"energy": jnp.minimum(me + 1, ne - 1)}))
    pl.when(has_prev)(lambda: greet({"energy": jnp.maximum(me - 1, 0)}))
    greet({"seg": partner})
    pl.when(far_out)(lambda: greet({"seg": far_to}))
    pl.when(far_in)(lambda: greet({"seg": far_from}))

    def greet_part(k, carry):
        greet({"energy": lax.rem(chip + k, half) * 2 + core})
        return carry

    lax.fori_loop(1, half, greet_part, 0)
    for load in loads:
        load.start()

    @pl.when(jnp.logical_not(has_prev))
    def _():
        win[:, :width] = jnp.zeros((3, width) + win.shape[2:], BF16)

    @pl.when(jnp.logical_not(has_next))
    def _():
        win[:, 2 * width :] = jnp.zeros((3, width) + win.shape[2:], BF16)

    @pl.when(jnp.logical_not(far_in))
    def _():
        win[far] = jnp.zeros(win.shape[1:], BF16)

    loads[0].wait()
    loads[-1].wait()
    for e in range(width):
        own = raw[e]
        win[1, width + e] = jnp.where(e < counts[0], own, jnp.zeros_like(own))

    total = 1 + half - 1
    for cond in (has_next, has_prev, far_out, far_in):
        total = total + cond.astype(jnp.int32)
    pl.semaphore_wait(barrier, total)

    for k, j in chunks:
        s_copy(0, k, j).start()
        for way in range(2):
            pl.when(e_out[way])(lambda: e_copy(way, 0, k, j).start())

    for load in loads[1:-1]:
        load.wait()
    for n in range(nbr):
        re, im = coup[n, 0], coup[n, 1]
        coup_a[n, :size, :size] = re
        coup_a[n, :size, size:] = -im
        coup_a[n, size:, :size] = im
        coup_a[n, size:, size:] = re
        at = 2 * n * size
        coup_b[:size, at : at + size] = re
        coup_b[:size, at + size : at + 2 * size] = im
        coup_b[size:, at : at + size] = -im
        coup_b[size:, at + size : at + 2 * size] = re

    def pass_near(k, j):
        s_copy(0, k, j).wait_recv()
        pl.when(far_out)(lambda: s_copy(1, k, j).start())
        for way in range(2):
            pl.when(e_out[way])(lambda: e_copy(way, 1, k, j).start())

    def pass_far(k, j):
        @pl.when(far_in)
        def _():
            s_copy(1, k, j).wait_recv()
            for way in range(2):
                pl.when(e_out[way])(lambda: e_copy(way, 2, k, j).start())

    def pair(e, p):
        return jnp.concatenate([win[1, e, p], win[1, e, p + 1]], axis=1)

    to_sibling = pltpu.make_async_remote_copy(
        src_ref=pair_tx,
        dst_ref=pair_rx,
        send_sem=pair_sem.at[0],
        recv_sem=pair_sem.at[1],
        device_id={"energy": sibling},
        device_id_type=mesh_type,
    )

    def own_polar():
        total = None
        for e in range(width):
            lower = jnp.concatenate(
                [pair(width + e + d, 0) for d in range(1, width + 1)], axis=0
            )
            re, im = win[1, width + e, 2], win[1, width + e, 3]
            upper = jnp.concatenate(
                [
                    jnp.concatenate([re, im], axis=1),
                    jnp.concatenate([-im, re], axis=1),
                ],
                axis=0,
            )
            term = lax.dot_general(lower, upper, NT, preferred_element_type=F32)
            total = term if total is None else total + term
        for m in range(noff):
            chosen = total[:size]
            for d in range(2, width + 1):
                chosen = jnp.where(
                    offsets[m] == d, total[(d - 1) * size : d * size], chosen
                )
            pol[2 * m * size : (2 * m + 1) * size] = chosen[:, :size]
            pol[(2 * m + 1) * size : (2 * m + 2) * size] = chosen[:, size:]
        padded = slabs.shape[1]
        for d in range(ne):
            if padded > rows:
                slabs[d, rows:] = jnp.zeros((padded - rows, size), F32)
            slabs[d, :rows] = pol[d * rows : (d + 1) * rows]

        def fill(q, carry):
            pair_tx[q] = slabs[2 * q + 1 - core].astype(BF16)
            return carry

        lax.fori_loop(0, half, fill, 0)
        to_sibling.start()

    def part_copy(k):
        there = lax.rem(chip + k, half)
        return pltpu.make_async_remote_copy(
            src_ref=part_tx.at[there],
            dst_ref=part_rx.at[chip],
            send_sem=part_send.at[k],
            recv_sem=part_recv.at[k],
            device_id={"energy": there * 2 + core},
            device_id_type=mesh_type,
        )

    def send_part(k, carry):
        there = lax.rem(chip + k, half)
        value = slabs[2 * there + core] + pair_rx[there].astype(F32)
        part_tx[there] = value.astype(BF16)
        part_copy(k).start()
        return carry

    pass_near(*chunks[0])
    for j in range(width):
        pl.when(e_in[1])(lambda: e_copy(1, 0, 0, j).wait_recv())
    own_polar()
    for i in range(1, len(chunks)):
        pass_near(*chunks[i])
        pass_far(*chunks[i - 1])
    pass_far(*chunks[-1])
    to_sibling.wait_recv()
    lax.fori_loop(1, half, send_part, 0)

    weights = []
    for n in range(nbr):
        up, down = [None], [None]
        for d in range(1, width + 1):
            a = b = jnp.float32(0)
            for m in range(noff):
                hit = offsets[m] == d
                a = a + jnp.where(hit, phonon[0, m, 0, n], 0.0)
                b = b + jnp.where(hit, phonon[0, m, 1, n], 0.0)
            up.append(a)
            down.append(b)
        weights.append((up, down))

    tile = 16
    for k in range(2):
        for kind in range(3):
            for way in range(2):
                for j in range(width):
                    if (kind, way, k) == (0, 1, 0):
                        continue
                    cond = e_in[way]
                    if kind == 2:
                        cond = jnp.logical_and(cond, far_in)
                    pl.when(cond)(lambda: e_copy(way, kind, k, j).wait_recv())

        for ri in range(2):
            p = 2 * k + ri

            def mix(t, carry, p=p, k=k, ri=ri):
                r = pl.multiple_of(t * tile, tile)
                g = [
                    [win[c, e, p, pl.ds(r, tile), :] for e in range(3 * width)]
                    for c in range(3)
                ]
                for n in range(nbr):
                    to = neighbour[0, n]
                    chosen = [
                        jnp.where(
                            to == 0, g[1][e], jnp.where(to < 0, g[0][e], g[2][e])
                        ).astype(F32)
                        for e in range(3 * width)
                    ]
                    up, down = weights[n] if k == 0 else weights[n][::-1]
                    for e in range(width):
                        acc = None
                        for d in range(1, width + 1):
                            term = (
                                up[d] * chosen[width + e + d]
                                + down[d] * chosen[width + e - d]
                            )
                            acc = term if acc is None else acc + term
                        at = (k * width + e) * size
                        mixed[n, pl.ds(ri * size + r, tile), at : at + size] = (
                            acc.astype(BF16)
                        )
                return carry

            lax.fori_loop(0, size // tile, mix, 0)

        first = k * width * size
        for n in range(nbr):
            y = lax.dot_general(
                coup_a[n],
                mixed[n, :, first : first + width * size],
                NN,
                preferred_element_type=F32,
            ).astype(BF16)
            for e in range(width):
                for ri in range(2):
                    at = (2 * n + ri) * size
                    left[first + e * size : first + (e + 1) * size, at : at + size] = y[
                        ri * size : (ri + 1) * size, e * size : (e + 1) * size
                    ]
        for e in range(width):
            out = lax.dot_general(
                left[first + e * size : first + (e + 1) * size],
                coup_b[...],
                NT,
                preferred_element_type=F32,
            )
            sigma[e, 0, 2 * k] = out[:, :size]
            sigma[e, 0, 2 * k + 1] = out[:, size:]
        stores[k].start()

    def wait_part(k, carry):
        part_copy(k).wait()
        return carry

    lax.fori_loop(1, half, wait_part, 0)
    mine = slabs[me] + pair_rx[chip].astype(F32)

    def add_part(k, acc):
        return acc + part_rx[lax.rem(chip + k, half)].astype(F32)

    mine = lax.fori_loop(1, half, add_part, mine)
    polar[0] = mine[:rows]
    stores[2].start()

    to_sibling.wait_send()
    for k, j in chunks:
        s_copy(0, k, j).wait_send()
        pl.when(far_out)(lambda: s_copy(1, k, j).wait_send())
        for way in range(2):
            for kind in range(3):
                cond = e_out[way]
                if kind == 2:
                    cond = jnp.logical_and(cond, far_in)
                pl.when(cond)(lambda: e_copy(way, kind, k, j).wait_send())
    for store in stores:
        store.wait()


def deliver(sigma_in, polar_in, sigma, polar, sems):
    moves = [
        pltpu.make_async_copy(sigma_in, sigma, sems.at[0]),
        pltpu.make_async_copy(polar_in, polar, sems.at[1]),
    ]
    for move in moves:
        move.start()
    for move in moves:
        move.wait()


def local(ne, ns, green, couple, phonon, neighbour, offsets, counts):
    width, size = green.shape[0], green.shape[-1]
    nbr, noff = couple.shape[1], phonon.shape[2]
    rows = 2 * noff * size // ne
    padded = -(-rows // 16) * 16
    half = ne // 2
    hbm = pl.BlockSpec(memory_space=pltpu.HBM)
    dma = pltpu.SemaphoreType.DMA
    results = (
        jax.ShapeDtypeStruct(green.shape, F32),
        jax.ShapeDtypeStruct((1, rows, size), F32),
    )
    phonon = jnp.transpose(phonon, (0, 2, 3, 1))
    found = pl.pallas_call(
        functools.partial(kernel, ne, ns),
        out_shape=results,
        in_specs=[hbm] * 6,
        out_specs=(hbm, hbm),
        scratch_shapes=[
            pltpu.SMEM(phonon.shape, F32),
            pltpu.SMEM(neighbour.shape, jnp.int32),
            pltpu.SMEM(offsets.shape, jnp.int32),
            pltpu.SMEM(counts.shape, jnp.int32),
            pltpu.VMEM(green.shape, F32),
            pltpu.VMEM((1, rows, size), F32),
            pltpu.VMEM((width, 4, size, size), BF16),
            pltpu.VMEM((nbr, 2, size, size), BF16),
            pltpu.VMEM((3, 3 * width, 4, size, size), BF16),
            pltpu.VMEM((nbr, 2 * size, 2 * width * size), BF16),
            pltpu.VMEM((2 * width * size, 2 * nbr * size), BF16),
            pltpu.VMEM((nbr, 2 * size, 2 * size), BF16),
            pltpu.VMEM((2 * size, 2 * nbr * size), BF16),
            pltpu.VMEM((2 * noff * size, size), F32),
            pltpu.VMEM((ne, padded, size), F32),
            pltpu.VMEM((half, padded, size), BF16),
            pltpu.VMEM((half, padded, size), BF16),
            pltpu.VMEM((half, padded, size), BF16),
            pltpu.VMEM((half, padded, size), BF16),
            dma((6,)),
            dma((2, 3, 2, width)),
            dma((2, 3, 2, width)),
            dma((2, 2, width)),
            dma((2, 2, width)),
            dma((2,)),
            dma((half,)),
            dma((half,)),
            dma((3,)),
        ],
        compiler_params=pltpu.CompilerParams(
            collective_id=0, has_side_effects=True, vmem_limit_bytes=60 * 1024 * 1024
        ),
        cost_estimate=pl.CostEstimate(
            flops=600_000_000, bytes_accessed=4_000_000, transcendentals=0
        ),
    )(phonon, neighbour, offsets, counts, green, couple)
    return pl.pallas_call(
        deliver,
        out_shape=results,
        in_specs=[hbm] * 2,
        out_specs=(hbm, hbm),
        scratch_shapes=[dma((2,))],
        compiler_params=pltpu.CompilerParams(vmem_limit_bytes=60 * 1024 * 1024),
    )(*found)


def solution(mesh):
    placed = (
        P("energy", "seg", None, None, None),
        P("seg", None, None, None, None),
        P("seg", None, None, None),
        P("seg", None),
        P(),
        P("energy"),
    )
    return jax.shard_map(
        functools.partial(local, mesh.shape["energy"], mesh.shape["seg"]),
        mesh=mesh,
        in_specs=placed,
        out_specs=(P("energy", "seg", None, None, None), P("seg", "energy", None)),
        check_vma=False,
    )
```

```python
import functools

import jax
import jax.numpy as jnp
from jax import lax
from jax.experimental import pallas as pl
from jax.experimental.pallas import tpu as pltpu
from jax.sharding import PartitionSpec as P

F32 = jnp.float32
BF16 = jnp.bfloat16
NT = (((1,), (1,)), ((), ()))
NN = (((1,), (0,)), ((), ()))


def kernel(
    ne,
    ns,
    phonon_in,
    neighbour_in,
    offsets_in,
    counts_in,
    green,
    couple,
    sigma_out,
    polar_out,
    phonon,
    neighbour,
    offsets,
    counts,
    sigma,
    polar,
    raw,
    coup,
    win,
    mixed,
    left,
    coup_a,
    coup_b,
    pol,
    slabs,
    pair_tx,
    pair_rx,
    part_tx,
    part_rx,
    load_sem,
    e_send,
    e_recv,
    s_send,
    s_recv,
    pair_sem,
    part_send,
    part_recv,
    out_sem,
):
    width, size = green.shape[0], green.shape[-1]
    nbr, noff = couple.shape[1], phonon_in.shape[1]
    rows = polar.shape[1]
    half = ne // 2
    me, seg = lax.axis_index("energy"), lax.axis_index("seg")
    core, chip = lax.rem(me, 2), lax.div(me, 2)
    sibling = me + 1 - 2 * core
    side = lax.rem(seg, 2)
    has_next, has_prev = me < ne - 1, me > 0
    partner = seg + 1 - 2 * side
    above, below = seg + 2 < ns, seg >= 2
    even = side == 0
    far_out = jnp.logical_or(
        jnp.logical_and(even, above), jnp.logical_and(jnp.logical_not(even), below)
    )
    far_in = jnp.logical_or(
        jnp.logical_and(even, below), jnp.logical_and(jnp.logical_not(even), above)
    )
    far_to = jnp.clip(seg + 2 - 4 * side, 0, ns - 1)
    far_from = jnp.clip(seg - 2 + 4 * side, 0, ns - 1)
    near, far = 2 - 2 * side, 2 * side
    slots = (1, near, far)
    mesh_type = pl.DeviceIdType.MESH
    chunks = [(k, j) for k in range(2) for j in range(width)]

    loads = [
        pltpu.make_async_copy(green.at[:, 0], raw, load_sem.at[0]),
        pltpu.make_async_copy(couple.at[0], coup, load_sem.at[1]),
        pltpu.make_async_copy(phonon_in, phonon, load_sem.at[2]),
        pltpu.make_async_copy(neighbour_in, neighbour, load_sem.at[3]),
        pltpu.make_async_copy(offsets_in, offsets, load_sem.at[4]),
        pltpu.make_async_copy(counts_in, counts, load_sem.at[5]),
    ]
    stores = [
        pltpu.make_async_copy(
            sigma.at[:, :, pl.ds(2 * k, 2)],
            sigma_out.at[:, :, pl.ds(2 * k, 2)],
            out_sem.at[k],
        )
        for k in range(2)
    ]
    stores.append(pltpu.make_async_copy(polar, polar_out, out_sem.at[2]))

    def e_copy(way, kind, k, j):
        there = jnp.minimum(me + 1, ne - 1) if way == 0 else jnp.maximum(me - 1, 0)
        return pltpu.make_async_remote_copy(
            src_ref=win.at[slots[kind], width + j, pl.ds(2 * k, 2)],
            dst_ref=win.at[slots[kind], 2 * width * way + j, pl.ds(2 * k, 2)],
            send_sem=e_send.at[way, kind, k, j],
            recv_sem=e_recv.at[way, kind, k, j],
            device_id={"energy": there},
            device_id_type=mesh_type,
        )

    def s_copy(kind, k, j):
        return pltpu.make_async_remote_copy(
            src_ref=win.at[1 if kind == 0 else near, width + j, pl.ds(2 * k, 2)],
            dst_ref=win.at[far, width + j, pl.ds(2 * k, 2)],
            send_sem=s_send.at[kind, k, j],
            recv_sem=s_recv.at[kind, k, j],
            device_id={"seg": partner if kind == 0 else far_to},
            device_id_type=mesh_type,
        )

    e_out, e_in = (has_next, has_prev), (has_prev, has_next)

    barrier = pltpu.get_barrier_semaphore()

    def greet(where):
        pl.semaphore_signal(barrier, inc=1, device_id=where, device_id_type=mesh_type)

    pl.when(has_next)(lambda: greet({"energy": jnp.minimum(me + 1, ne - 1)}))
    pl.when(has_prev)(lambda: greet({"energy": jnp.maximum(me - 1, 0)}))
    greet({"seg": partner})
    pl.when(far_out)(lambda: greet({"seg": far_to}))
    pl.when(far_in)(lambda: greet({"seg": far_from}))

    def greet_part(k, carry):
        greet({"energy": lax.rem(chip + k, half) * 2 + core})
        return carry

    lax.fori_loop(1, half, greet_part, 0)
    for load in loads:
        load.start()

    @pl.when(jnp.logical_not(has_prev))
    def _():
        win[:, :width] = jnp.zeros((3, width) + win.shape[2:], BF16)

    @pl.when(jnp.logical_not(has_next))
    def _():
        win[:, 2 * width :] = jnp.zeros((3, width) + win.shape[2:], BF16)

    @pl.when(jnp.logical_not(far_in))
    def _():
        win[far] = jnp.zeros(win.shape[1:], BF16)

    loads[0].wait()
    loads[-1].wait()
    for e in range(width):
        own = raw[e]
        win[1, width + e] = jnp.where(e < counts[0], own, jnp.zeros_like(own))

    total = 1 + half - 1
    for cond in (has_next, has_prev, far_out, far_in):
        total = total + cond.astype(jnp.int32)
    pl.semaphore_wait(barrier, total)

    for k, j in chunks:
        s_copy(0, k, j).start()
        for way in range(2):
            pl.when(e_out[way])(lambda: e_copy(way, 0, k, j).start())

    for load in loads[1:-1]:
        load.wait()
    for n in range(nbr):
        re, im = coup[n, 0], coup[n, 1]
        coup_a[n, :size, :size] = re
        coup_a[n, :size, size:] = -im
        coup_a[n, size:, :size] = im
        coup_a[n, size:, size:] = re
        at = 2 * n * size
        coup_b[:size, at : at + size] = re
        coup_b[:size, at + size : at + 2 * size] = im
        coup_b[size:, at : at + size] = -im
        coup_b[size:, at + size : at + 2 * size] = re

    def pass_near(k, j):
        s_copy(0, k, j).wait_recv()
        pl.when(far_out)(lambda: s_copy(1, k, j).start())
        for way in range(2):
            pl.when(e_out[way])(lambda: e_copy(way, 1, k, j).start())

    def pass_far(k, j):
        @pl.when(far_in)
        def _():
            s_copy(1, k, j).wait_recv()
            for way in range(2):
                pl.when(e_out[way])(lambda: e_copy(way, 2, k, j).start())

    def pair(e, p):
        return jnp.concatenate([win[1, e, p], win[1, e, p + 1]], axis=1)

    to_sibling = pltpu.make_async_remote_copy(
        src_ref=pair_tx,
        dst_ref=pair_rx,
        send_sem=pair_sem.at[0],
        recv_sem=pair_sem.at[1],
        device_id={"energy": sibling},
        device_id_type=mesh_type,
    )

    def own_polar():
        total = None
        for e in range(width):
            lower = jnp.concatenate(
                [pair(width + e + d, 0) for d in range(1, width + 1)], axis=0
            )
            re, im = win[1, width + e, 2], win[1, width + e, 3]
            upper = jnp.concatenate(
                [
                    jnp.concatenate([re, im], axis=1),
                    jnp.concatenate([-im, re], axis=1),
                ],
                axis=0,
            )
            term = lax.dot_general(lower, upper, NT, preferred_element_type=F32)
            total = term if total is None else total + term
        for m in range(noff):
            chosen = total[:size]
            for d in range(2, width + 1):
                chosen = jnp.where(
                    offsets[m] == d, total[(d - 1) * size : d * size], chosen
                )
            pol[2 * m * size : (2 * m + 1) * size] = chosen[:, :size]
            pol[(2 * m + 1) * size : (2 * m + 2) * size] = chosen[:, size:]
        padded = slabs.shape[1]
        for d in range(ne):
            if padded > rows:
                slabs[d, rows:] = jnp.zeros((padded - rows, size), F32)
            slabs[d, :rows] = pol[d * rows : (d + 1) * rows]

        def fill(q, carry):
            pair_tx[q] = slabs[2 * q + 1 - core].astype(BF16)
            return carry

        lax.fori_loop(0, half, fill, 0)
        to_sibling.start()

    def part_copy(k):
        there = lax.rem(chip + k, half)
        return pltpu.make_async_remote_copy(
            src_ref=part_tx.at[there],
            dst_ref=part_rx.at[chip],
            send_sem=part_send.at[k],
            recv_sem=part_recv.at[k],
            device_id={"energy": there * 2 + core},
            device_id_type=mesh_type,
        )

    def send_part(k, carry):
        there = lax.rem(chip + k, half)
        value = slabs[2 * there + core] + pair_rx[there].astype(F32)
        part_tx[there] = value.astype(BF16)
        part_copy(k).start()
        return carry

    ahead = 2
    for i in range(len(chunks)):
        pass_near(*chunks[i])
        if i >= ahead:
            pass_far(*chunks[i - ahead])
    for j in range(width):
        pl.when(e_in[1])(lambda: e_copy(1, 0, 0, j).wait_recv())
    own_polar()
    for i in range(len(chunks) - ahead, len(chunks)):
        pass_far(*chunks[i])
    to_sibling.wait_recv()
    lax.fori_loop(1, half, send_part, 0)

    weights = []
    for n in range(nbr):
        up, down = [None], [None]
        for d in range(1, width + 1):
            a = b = jnp.float32(0)
            for m in range(noff):
                hit = offsets[m] == d
                a = a + jnp.where(hit, phonon[0, m, 0, n], 0.0)
                b = b + jnp.where(hit, phonon[0, m, 1, n], 0.0)
            up.append(a)
            down.append(b)
        weights.append((up, down))

    tile = 16
    for k in range(2):
        for kind in range(3):
            for way in range(2):
                for j in range(width):
                    if (kind, way, k) == (0, 1, 0):
                        continue
                    cond = e_in[way]
                    if kind == 2:
                        cond = jnp.logical_and(cond, far_in)
                    pl.when(cond)(lambda: e_copy(way, kind, k, j).wait_recv())

        for ri in range(2):
            p = 2 * k + ri

            def mix(t, carry, p=p, k=k, ri=ri):
                r = pl.multiple_of(t * tile, tile)
                g = [
                    [win[c, e, p, pl.ds(r, tile), :] for e in range(3 * width)]
                    for c in range(3)
                ]
                for n in range(nbr):
                    to = neighbour[0, n]
                    chosen = [
                        jnp.where(
                            to == 0, g[1][e], jnp.where(to < 0, g[0][e], g[2][e])
                        ).astype(F32)
                        for e in range(3 * width)
                    ]
                    up, down = weights[n] if k == 0 else weights[n][::-1]
                    for e in range(width):
                        acc = None
                        for d in range(1, width + 1):
                            term = (
                                up[d] * chosen[width + e + d]
                                + down[d] * chosen[width + e - d]
                            )
                            acc = term if acc is None else acc + term
                        at = (k * width + e) * size
                        mixed[n, pl.ds(ri * size + r, tile), at : at + size] = (
                            acc.astype(BF16)
                        )
                return carry

            lax.fori_loop(0, size // tile, mix, 0)

        first = k * width * size
        for n in range(nbr):
            y = lax.dot_general(
                coup_a[n],
                mixed[n, :, first : first + width * size],
                NN,
                preferred_element_type=F32,
            ).astype(BF16)
            for e in range(width):
                for ri in range(2):
                    at = (2 * n + ri) * size
                    left[first + e * size : first + (e + 1) * size, at : at + size] = y[
                        ri * size : (ri + 1) * size, e * size : (e + 1) * size
                    ]
        for e in range(width):
            out = lax.dot_general(
                left[first + e * size : first + (e + 1) * size],
                coup_b[...],
                NT,
                preferred_element_type=F32,
            )
            sigma[e, 0, 2 * k] = out[:, :size]
            sigma[e, 0, 2 * k + 1] = out[:, size:]
        stores[k].start()

    def wait_part(k, carry):
        part_copy(k).wait()
        return carry

    lax.fori_loop(1, half, wait_part, 0)
    mine = slabs[me] + pair_rx[chip].astype(F32)

    def add_part(k, acc):
        return acc + part_rx[lax.rem(chip + k, half)].astype(F32)

    mine = lax.fori_loop(1, half, add_part, mine)
    polar[0] = mine[:rows]
    stores[2].start()

    to_sibling.wait_send()
    for k, j in chunks:
        s_copy(0, k, j).wait_send()
        pl.when(far_out)(lambda: s_copy(1, k, j).wait_send())
        for way in range(2):
            for kind in range(3):
                cond = e_out[way]
                if kind == 2:
                    cond = jnp.logical_and(cond, far_in)
                pl.when(cond)(lambda: e_copy(way, kind, k, j).wait_send())
    for store in stores:
        store.wait()


def local(ne, ns, green, couple, phonon, neighbour, offsets, counts):
    width, size = green.shape[0], green.shape[-1]
    nbr, noff = couple.shape[1], phonon.shape[2]
    rows = 2 * noff * size // ne
    padded = -(-rows // 16) * 16
    half = ne // 2
    hbm = pl.BlockSpec(memory_space=pltpu.HBM)
    dma = pltpu.SemaphoreType.DMA
    results = (
        jax.ShapeDtypeStruct(green.shape, F32),
        jax.ShapeDtypeStruct((1, rows, size), F32),
    )
    phonon = jnp.transpose(phonon, (0, 2, 3, 1))
    return pl.pallas_call(
        functools.partial(kernel, ne, ns),
        out_shape=results,
        in_specs=[hbm] * 6,
        out_specs=(hbm, hbm),
        scratch_shapes=[
            pltpu.SMEM(phonon.shape, F32),
            pltpu.SMEM(neighbour.shape, jnp.int32),
            pltpu.SMEM(offsets.shape, jnp.int32),
            pltpu.SMEM(counts.shape, jnp.int32),
            pltpu.VMEM(green.shape, F32),
            pltpu.VMEM((1, rows, size), F32),
            pltpu.VMEM((width, 4, size, size), BF16),
            pltpu.VMEM((nbr, 2, size, size), BF16),
            pltpu.VMEM((3, 3 * width, 4, size, size), BF16),
            pltpu.VMEM((nbr, 2 * size, 2 * width * size), BF16),
            pltpu.VMEM((2 * width * size, 2 * nbr * size), BF16),
            pltpu.VMEM((nbr, 2 * size, 2 * size), BF16),
            pltpu.VMEM((2 * size, 2 * nbr * size), BF16),
            pltpu.VMEM((2 * noff * size, size), F32),
            pltpu.VMEM((ne, padded, size), F32),
            pltpu.VMEM((half, padded, size), BF16),
            pltpu.VMEM((half, padded, size), BF16),
            pltpu.VMEM((half, padded, size), BF16),
            pltpu.VMEM((half, padded, size), BF16),
            dma((6,)),
            dma((2, 3, 2, width)),
            dma((2, 3, 2, width)),
            dma((2, 2, width)),
            dma((2, 2, width)),
            dma((2,)),
            dma((half,)),
            dma((half,)),
            dma((3,)),
        ],
        compiler_params=pltpu.CompilerParams(
            collective_id=0, has_side_effects=True, vmem_limit_bytes=60 * 1024 * 1024
        ),
        cost_estimate=pl.CostEstimate(
            flops=600_000_000, bytes_accessed=4_000_000, transcendentals=0
        ),
    )(phonon, neighbour, offsets, counts, green, couple)


def solution(mesh):
    placed = (
        P("energy", "seg", None, None, None),
        P("seg", None, None, None, None),
        P("seg", None, None, None),
        P("seg", None),
        P(),
        P("energy"),
    )
    return jax.shard_map(
        functools.partial(local, mesh.shape["energy"], mesh.shape["seg"]),
        mesh=mesh,
        in_specs=placed,
        out_specs=(P("energy", "seg", None, None, None), P("seg", "energy", None)),
        check_vma=False,
    )
```

```python
import functools

import jax
import jax.numpy as jnp
from jax import lax
from jax.experimental import pallas as pl
from jax.experimental.pallas import tpu as pltpu
from jax.sharding import PartitionSpec as P

F32 = jnp.float32
BF16 = jnp.bfloat16
NT = (((1,), (1,)), ((), ()))
NN = (((1,), (0,)), ((), ()))


def kernel(
    ne,
    ns,
    phonon_in,
    neighbour_in,
    offsets_in,
    counts_in,
    green,
    couple,
    sigma_out,
    polar_out,
    phonon,
    neighbour,
    offsets,
    counts,
    sigma,
    polar,
    raw,
    coup,
    win,
    mixed,
    left,
    coup_a,
    coup_b,
    pol,
    slabs,
    pair_tx,
    pair_rx,
    part_tx,
    part_rx,
    load_sem,
    e_send,
    e_recv,
    s_send,
    s_recv,
    pair_sem,
    part_send,
    part_recv,
    out_sem,
):
    width, size = green.shape[0], green.shape[-1]
    nbr, noff = couple.shape[1], phonon_in.shape[1]
    rows = polar.shape[1]
    half = ne // 2
    me, seg = lax.axis_index("energy"), lax.axis_index("seg")
    core, chip = lax.rem(me, 2), lax.div(me, 2)
    sibling = me + 1 - 2 * core
    side = lax.rem(seg, 2)
    has_next, has_prev = me < ne - 1, me > 0
    partner = seg + 1 - 2 * side
    above, below = seg + 2 < ns, seg >= 2
    even = side == 0
    far_out = jnp.logical_or(
        jnp.logical_and(even, above), jnp.logical_and(jnp.logical_not(even), below)
    )
    far_in = jnp.logical_or(
        jnp.logical_and(even, below), jnp.logical_and(jnp.logical_not(even), above)
    )
    far_to = jnp.clip(seg + 2 - 4 * side, 0, ns - 1)
    far_from = jnp.clip(seg - 2 + 4 * side, 0, ns - 1)
    near, far = 2 - 2 * side, 2 * side
    slots = (1, near, far)
    mesh_type = pl.DeviceIdType.MESH
    chunks = [(k, j) for k in range(2) for j in range(width)]

    loads = [
        pltpu.make_async_copy(green.at[:, 0], raw, load_sem.at[0]),
        pltpu.make_async_copy(couple.at[0], coup, load_sem.at[1]),
        pltpu.make_async_copy(phonon_in, phonon, load_sem.at[2]),
        pltpu.make_async_copy(neighbour_in, neighbour, load_sem.at[3]),
        pltpu.make_async_copy(offsets_in, offsets, load_sem.at[4]),
        pltpu.make_async_copy(counts_in, counts, load_sem.at[5]),
    ]
    stores = [
        pltpu.make_async_copy(
            sigma.at[:, :, pl.ds(2 * k, 2)],
            sigma_out.at[:, :, pl.ds(2 * k, 2)],
            out_sem.at[k],
        )
        for k in range(2)
    ]
    stores.append(pltpu.make_async_copy(polar, polar_out, out_sem.at[2]))

    def e_copy(way, kind, k, j):
        there = jnp.minimum(me + 1, ne - 1) if way == 0 else jnp.maximum(me - 1, 0)
        return pltpu.make_async_remote_copy(
            src_ref=win.at[slots[kind], width + j, pl.ds(2 * k, 2)],
            dst_ref=win.at[slots[kind], 2 * width * way + j, pl.ds(2 * k, 2)],
            send_sem=e_send.at[way, kind, k, j],
            recv_sem=e_recv.at[way, kind, k, j],
            device_id={"energy": there},
            device_id_type=mesh_type,
        )

    def s_copy(kind, k, j):
        return pltpu.make_async_remote_copy(
            src_ref=win.at[1 if kind == 0 else near, width + j, pl.ds(2 * k, 2)],
            dst_ref=win.at[far, width + j, pl.ds(2 * k, 2)],
            send_sem=s_send.at[kind, k, j],
            recv_sem=s_recv.at[kind, k, j],
            device_id={"seg": partner if kind == 0 else far_to},
            device_id_type=mesh_type,
        )

    e_out, e_in = (has_next, has_prev), (has_prev, has_next)

    barrier = pltpu.get_barrier_semaphore()

    def greet(where):
        pl.semaphore_signal(barrier, inc=1, device_id=where, device_id_type=mesh_type)

    pl.when(has_next)(lambda: greet({"energy": jnp.minimum(me + 1, ne - 1)}))
    pl.when(has_prev)(lambda: greet({"energy": jnp.maximum(me - 1, 0)}))
    greet({"seg": partner})
    pl.when(far_out)(lambda: greet({"seg": far_to}))
    pl.when(far_in)(lambda: greet({"seg": far_from}))

    def greet_part(k, carry):
        greet({"energy": lax.rem(chip + k, half) * 2 + core})
        return carry

    lax.fori_loop(1, half, greet_part, 0)
    for load in loads:
        load.start()

    @pl.when(jnp.logical_not(has_prev))
    def _():
        win[:, :width] = jnp.zeros((3, width) + win.shape[2:], BF16)

    @pl.when(jnp.logical_not(has_next))
    def _():
        win[:, 2 * width :] = jnp.zeros((3, width) + win.shape[2:], BF16)

    @pl.when(jnp.logical_not(far_in))
    def _():
        win[far] = jnp.zeros(win.shape[1:], BF16)

    loads[0].wait()
    loads[-1].wait()
    for e in range(width):
        own = raw[e]
        win[1, width + e] = jnp.where(e < counts[0], own, jnp.zeros_like(own))

    total = 1 + half - 1
    for cond in (has_next, has_prev, far_out, far_in):
        total = total + cond.astype(jnp.int32)
    pl.semaphore_wait(barrier, total)

    for k, j in chunks:
        s_copy(0, k, j).start()
        for way in range(2):
            pl.when(e_out[way])(lambda: e_copy(way, 0, k, j).start())

    for load in loads[1:-1]:
        load.wait()
    values = (jnp.int32(0), 1 - 2 * side, 2 * side - 1)
    picks = []
    for value in values:
        pick = jnp.int32(nbr - 1)
        for n in range(nbr - 2, -1, -1):
            pick = jnp.where(neighbour[0, n] == value, n, pick)
        picks.append(pick)
    extra = nbr * (nbr - 1) // 2 - picks[0] - picks[1] - picks[2]
    picks.append(extra)
    extra_to = neighbour[0, extra]
    weights = []
    for i, pick in enumerate(picks):
        up, down = [None], [None]
        for d in range(1, width + 1):
            a = b = jnp.float32(0)
            for m in range(noff):
                hit = offsets[m] == d
                a = a + jnp.where(hit, phonon[0, m, 0, pick], 0.0)
                b = b + jnp.where(hit, phonon[0, m, 1, pick], 0.0)
            up.append(a)
            down.append(b)
        weights.append((up, down))
        re, im = coup[pick, 0], coup[pick, 1]
        coup_a[i, :size, :size] = re
        coup_a[i, :size, size:] = -im
        coup_a[i, size:, :size] = im
        coup_a[i, size:, size:] = re
        at = 2 * i * size
        coup_b[:size, at : at + size] = re
        coup_b[:size, at + size : at + 2 * size] = im
        coup_b[size:, at : at + size] = -im
        coup_b[size:, at + size : at + 2 * size] = re

    def pass_near(k, j):
        s_copy(0, k, j).wait_recv()
        pl.when(far_out)(lambda: s_copy(1, k, j).start())
        for way in range(2):
            pl.when(e_out[way])(lambda: e_copy(way, 1, k, j).start())

    def pass_far(k, j):
        @pl.when(far_in)
        def _():
            s_copy(1, k, j).wait_recv()
            for way in range(2):
                pl.when(e_out[way])(lambda: e_copy(way, 2, k, j).start())

    def pair(e, p):
        return jnp.concatenate([win[1, e, p], win[1, e, p + 1]], axis=1)

    to_sibling = pltpu.make_async_remote_copy(
        src_ref=pair_tx,
        dst_ref=pair_rx,
        send_sem=pair_sem.at[0],
        recv_sem=pair_sem.at[1],
        device_id={"energy": sibling},
        device_id_type=mesh_type,
    )

    def own_polar():
        total = None
        for e in range(width):
            lower = jnp.concatenate(
                [pair(width + e + d, 0) for d in range(1, width + 1)], axis=0
            )
            re, im = win[1, width + e, 2], win[1, width + e, 3]
            upper = jnp.concatenate(
                [
                    jnp.concatenate([re, im], axis=1),
                    jnp.concatenate([-im, re], axis=1),
                ],
                axis=0,
            )
            term = lax.dot_general(lower, upper, NT, preferred_element_type=F32)
            total = term if total is None else total + term
        for m in range(noff):
            chosen = total[:size]
            for d in range(2, width + 1):
                chosen = jnp.where(
                    offsets[m] == d, total[(d - 1) * size : d * size], chosen
                )
            pol[2 * m * size : (2 * m + 1) * size] = chosen[:, :size]
            pol[(2 * m + 1) * size : (2 * m + 2) * size] = chosen[:, size:]
        padded = slabs.shape[1]
        for d in range(ne):
            if padded > rows:
                slabs[d, rows:] = jnp.zeros((padded - rows, size), F32)
            slabs[d, :rows] = pol[d * rows : (d + 1) * rows]

        def fill(q, carry):
            pair_tx[q] = slabs[2 * q + 1 - core].astype(BF16)
            return carry

        lax.fori_loop(0, half, fill, 0)
        to_sibling.start()

    def part_copy(k):
        there = lax.rem(chip + k, half)
        return pltpu.make_async_remote_copy(
            src_ref=part_tx.at[there],
            dst_ref=part_rx.at[chip],
            send_sem=part_send.at[k],
            recv_sem=part_recv.at[k],
            device_id={"energy": there * 2 + core},
            device_id_type=mesh_type,
        )

    def send_part(k, carry):
        there = lax.rem(chip + k, half)
        value = slabs[2 * there + core] + pair_rx[there].astype(F32)
        part_tx[there] = value.astype(BF16)
        part_copy(k).start()
        return carry

    tile = 16

    def halo(kind, k, skip=()):
        for way in range(2):
            for j in range(width):
                if way in skip:
                    continue
                cond = e_in[way]
                if kind == 2:
                    cond = jnp.logical_and(cond, far_in)
                pl.when(cond)(lambda: e_copy(way, kind, k, j).wait_recv())

    def job(i, k):
        up, down = weights[i] if k == 0 else weights[i][::-1]
        for ri in range(2):
            p = 2 * k + ri

            def mix(t, carry, p=p, ri=ri):
                r = pl.multiple_of(t * tile, tile)

                def at_slot(slot):
                    return [
                        win[slot, e, p, pl.ds(r, tile), :] for e in range(3 * width)
                    ]

                if i < 3:
                    chosen = at_slot(slots[i])
                else:
                    g = [at_slot(c) for c in range(3)]
                    chosen = [
                        jnp.where(
                            extra_to == 0,
                            g[1][e],
                            jnp.where(extra_to < 0, g[0][e], g[2][e]),
                        )
                        for e in range(3 * width)
                    ]
                chosen = [c.astype(F32) for c in chosen]
                for e in range(width):
                    acc = None
                    for d in range(1, width + 1):
                        term = (
                            up[d] * chosen[width + e + d]
                            + down[d] * chosen[width + e - d]
                        )
                        acc = term if acc is None else acc + term
                    at = (k * width + e) * size
                    mixed[i, pl.ds(ri * size + r, tile), at : at + size] = acc.astype(
                        BF16
                    )
                return carry

            lax.fori_loop(0, size // tile, mix, 0)

        first = k * width * size
        y = lax.dot_general(
            coup_a[i],
            mixed[i, :, first : first + width * size],
            NN,
            preferred_element_type=F32,
        ).astype(BF16)
        for e in range(width):
            for ri in range(2):
                at = (2 * i + ri) * size
                left[first + e * size : first + (e + 1) * size, at : at + size] = y[
                    ri * size : (ri + 1) * size, e * size : (e + 1) * size
                ]

    def finish(k):
        first = k * width * size
        out = lax.dot_general(
            left[first : first + width * size],
            coup_b[...],
            NT,
            preferred_element_type=F32,
        )
        for e in range(width):
            for ri in range(2):
                sigma[e, 0, 2 * k + ri] = out[
                    e * size : (e + 1) * size, ri * size : (ri + 1) * size
                ]
        stores[k].start()

    last = len(chunks) - 1
    for i in range(len(chunks)):
        pass_near(*chunks[i])
        if i >= 2:
            pass_far(*chunks[i - 2])
        if i == last - 2:
            halo(0, 0)
            job(0, 0)
        if i == last - 1:
            halo(0, 1)
            job(0, 1)
    own_polar()
    pass_far(*chunks[last - 1])
    halo(1, 0)
    job(1, 0)
    pass_far(*chunks[last])
    to_sibling.wait_recv()
    lax.fori_loop(1, half, send_part, 0)
    halo(1, 1)
    job(1, 1)
    for k in range(2):
        halo(2, k)
        job(2, k)
        job(3, k)
        finish(k)

    def wait_part(k, carry):
        part_copy(k).wait()
        return carry

    lax.fori_loop(1, half, wait_part, 0)
    mine = slabs[me] + pair_rx[chip].astype(F32)

    def add_part(k, acc):
        return acc + part_rx[lax.rem(chip + k, half)].astype(F32)

    mine = lax.fori_loop(1, half, add_part, mine)
    polar[0] = mine[:rows]
    stores[2].start()

    to_sibling.wait_send()
    for k, j in chunks:
        s_copy(0, k, j).wait_send()
        pl.when(far_out)(lambda: s_copy(1, k, j).wait_send())
        for way in range(2):
            for kind in range(3):
                cond = e_out[way]
                if kind == 2:
                    cond = jnp.logical_and(cond, far_in)
                pl.when(cond)(lambda: e_copy(way, kind, k, j).wait_send())
    for store in stores:
        store.wait()


def deliver(sigma_in, polar_in, sigma, polar, sigma_at, polar_at, sems):
    width = sigma.shape[0]
    pieces = [
        (
            sigma_in.at[e, :, pl.ds(2 * k, 2)],
            sigma_at.at[e, :, pl.ds(2 * k, 2)],
            sigma.at[e, :, pl.ds(2 * k, 2)],
        )
        for k in range(2)
        for e in range(width)
    ]
    pieces.append((polar_in, polar_at, polar))
    ins = [
        pltpu.make_async_copy(a, b, sems.at[0, i]) for i, (a, b, _) in enumerate(pieces)
    ]
    outs = [
        pltpu.make_async_copy(b, c, sems.at[1, i]) for i, (_, b, c) in enumerate(pieces)
    ]
    for move in ins:
        move.start()
    for move, onward in zip(ins, outs):
        move.wait()
        onward.start()
    for onward in outs:
        onward.wait()


def local(ne, ns, green, couple, phonon, neighbour, offsets, counts):
    width, size = green.shape[0], green.shape[-1]
    nbr, noff = couple.shape[1], phonon.shape[2]
    rows = 2 * noff * size // ne
    padded = -(-rows // 16) * 16
    half = ne // 2
    hbm = pl.BlockSpec(memory_space=pltpu.HBM)
    dma = pltpu.SemaphoreType.DMA
    results = (
        jax.ShapeDtypeStruct(green.shape, F32),
        jax.ShapeDtypeStruct((1, rows, size), F32),
    )
    phonon = jnp.transpose(phonon, (0, 2, 3, 1))
    found = pl.pallas_call(
        functools.partial(kernel, ne, ns),
        out_shape=results,
        in_specs=[hbm] * 6,
        out_specs=(hbm, hbm),
        scratch_shapes=[
            pltpu.SMEM(phonon.shape, F32),
            pltpu.SMEM(neighbour.shape, jnp.int32),
            pltpu.SMEM(offsets.shape, jnp.int32),
            pltpu.SMEM(counts.shape, jnp.int32),
            pltpu.VMEM(green.shape, F32),
            pltpu.VMEM((1, rows, size), F32),
            pltpu.VMEM((width, 4, size, size), BF16),
            pltpu.VMEM((nbr, 2, size, size), BF16),
            pltpu.VMEM((3, 3 * width, 4, size, size), BF16),
            pltpu.VMEM((nbr, 2 * size, 2 * width * size), BF16),
            pltpu.VMEM((2 * width * size, 2 * nbr * size), BF16),
            pltpu.VMEM((nbr, 2 * size, 2 * size), BF16),
            pltpu.VMEM((2 * size, 2 * nbr * size), BF16),
            pltpu.VMEM((2 * noff * size, size), F32),
            pltpu.VMEM((ne, padded, size), F32),
            pltpu.VMEM((half, padded, size), BF16),
            pltpu.VMEM((half, padded, size), BF16),
            pltpu.VMEM((half, padded, size), BF16),
            pltpu.VMEM((half, padded, size), BF16),
            dma((6,)),
            dma((2, 3, 2, width)),
            dma((2, 3, 2, width)),
            dma((2, 2, width)),
            dma((2, 2, width)),
            dma((2,)),
            dma((half,)),
            dma((half,)),
            dma((3,)),
        ],
        compiler_params=pltpu.CompilerParams(
            collective_id=0, has_side_effects=True, vmem_limit_bytes=60 * 1024 * 1024
        ),
        cost_estimate=pl.CostEstimate(
            flops=600_000_000, bytes_accessed=4_000_000, transcendentals=0
        ),
    )(phonon, neighbour, offsets, counts, green, couple)
    return pl.pallas_call(
        deliver,
        out_shape=results,
        in_specs=[hbm] * 2,
        out_specs=(hbm, hbm),
        scratch_shapes=[
            pltpu.VMEM(green.shape, F32),
            pltpu.VMEM((1, rows, size), F32),
            dma((2, 2 * width + 1)),
        ],
        compiler_params=pltpu.CompilerParams(vmem_limit_bytes=60 * 1024 * 1024),
    )(*found)


def solution(mesh):
    placed = (
        P("energy", "seg", None, None, None),
        P("seg", None, None, None, None),
        P("seg", None, None, None),
        P("seg", None),
        P(),
        P("energy"),
    )
    return jax.shard_map(
        functools.partial(local, mesh.shape["energy"], mesh.shape["seg"]),
        mesh=mesh,
        in_specs=placed,
        out_specs=(P("energy", "seg", None, None, None), P("seg", "energy", None)),
        check_vma=False,
    )
```

```python
import functools

import jax
import jax.numpy as jnp
from jax import lax
from jax.experimental import pallas as pl
from jax.experimental.pallas import tpu as pltpu
from jax.sharding import PartitionSpec as P

F32 = jnp.float32
BF16 = jnp.bfloat16
NT = (((1,), (1,)), ((), ()))
NN = (((1,), (0,)), ((), ()))


def kernel(
    ne,
    ns,
    phonon_in,
    neighbour_in,
    offsets_in,
    counts_in,
    green,
    couple,
    sigma_out,
    polar_out,
    phonon,
    neighbour,
    offsets,
    counts,
    sigma,
    polar,
    raw,
    coup,
    win,
    mixed,
    left,
    coup_a,
    coup_b,
    pol,
    slabs,
    pair_tx,
    pair_rx,
    part_tx,
    part_rx,
    load_sem,
    e_send,
    e_recv,
    s_send,
    s_recv,
    pair_sem,
    part_send,
    part_recv,
    out_sem,
):
    width, size = green.shape[0], green.shape[-1]
    nbr, noff = couple.shape[1], phonon_in.shape[1]
    rows = polar.shape[1]
    half = ne // 2
    me, seg = lax.axis_index("energy"), lax.axis_index("seg")
    core, chip = lax.rem(me, 2), lax.div(me, 2)
    sibling = me + 1 - 2 * core
    side = lax.rem(seg, 2)
    has_next, has_prev = me < ne - 1, me > 0
    partner = seg + 1 - 2 * side
    above, below = seg + 2 < ns, seg >= 2
    even = side == 0
    far_out = jnp.logical_or(
        jnp.logical_and(even, above), jnp.logical_and(jnp.logical_not(even), below)
    )
    far_in = jnp.logical_or(
        jnp.logical_and(even, below), jnp.logical_and(jnp.logical_not(even), above)
    )
    far_to = jnp.clip(seg + 2 - 4 * side, 0, ns - 1)
    far_from = jnp.clip(seg - 2 + 4 * side, 0, ns - 1)
    across = jnp.clip(seg - 1 + 2 * side, 0, ns - 1)
    near, far = 2 - 2 * side, 2 * side
    slots = (1, near, far)
    mesh_type = pl.DeviceIdType.MESH
    chunks = [(k, j) for k in range(2) for j in range(width)]

    loads = [
        pltpu.make_async_copy(green.at[:, 0], raw, load_sem.at[0]),
        pltpu.make_async_copy(couple.at[0], coup, load_sem.at[1]),
        pltpu.make_async_copy(phonon_in, phonon, load_sem.at[2]),
        pltpu.make_async_copy(neighbour_in, neighbour, load_sem.at[3]),
        pltpu.make_async_copy(offsets_in, offsets, load_sem.at[4]),
        pltpu.make_async_copy(counts_in, counts, load_sem.at[5]),
    ]
    stores = [
        pltpu.make_async_copy(
            sigma.at[:, :, pl.ds(2 * k, 2)],
            sigma_out.at[:, :, pl.ds(2 * k, 2)],
            out_sem.at[k],
        )
        for k in range(2)
    ]
    stores.append(pltpu.make_async_copy(polar, polar_out, out_sem.at[2]))

    def e_move(way, kind, first, count, k, kinds):
        there = jnp.minimum(me + 1, ne - 1) if way == 0 else jnp.maximum(me - 1, 0)
        parts = pl.ds(2 * k, 2 * kinds)
        return pltpu.make_async_remote_copy(
            src_ref=win.at[slots[kind], pl.ds(width + first, count), parts],
            dst_ref=win.at[slots[kind], pl.ds(2 * width * way + first, count), parts],
            send_sem=e_send.at[way, kind],
            recv_sem=e_recv.at[way, kind, k],
            device_id={"energy": there},
            device_id_type=mesh_type,
        )

    def e_copy(way, kind, k, j):
        return e_move(way, kind, j, 1, k, 1)

    def s_copy(kind, k, j):
        return pltpu.make_async_remote_copy(
            src_ref=win.at[near if kind == 1 else 1, width + j, pl.ds(2 * k, 2)],
            dst_ref=win.at[near if kind == 2 else far, width + j, pl.ds(2 * k, 2)],
            send_sem=s_send.at[kind, k, j],
            recv_sem=s_recv.at[min(kind, 1), k, j],
            device_id={"seg": (partner, far_to, across)[kind]},
            device_id_type=mesh_type,
        )

    e_out, e_in = (has_next, has_prev), (has_prev, has_next)

    barrier = pltpu.get_barrier_semaphore()

    def greet(where):
        pl.semaphore_signal(barrier, inc=1, device_id=where, device_id_type=mesh_type)

    pl.when(has_next)(lambda: greet({"energy": jnp.minimum(me + 1, ne - 1)}))
    pl.when(has_prev)(lambda: greet({"energy": jnp.maximum(me - 1, 0)}))
    greet({"seg": partner})
    pl.when(far_out)(lambda: greet({"seg": far_to}))
    pl.when(far_in)(lambda: greet({"seg": far_from}))
    pl.when(far_in)(lambda: greet({"seg": across}))

    def greet_part(k, carry):
        greet({"energy": lax.rem(chip + k, half) * 2 + core})
        return carry

    lax.fori_loop(1, half, greet_part, 0)
    for load in loads:
        load.start()

    @pl.when(jnp.logical_not(has_prev))
    def _():
        win[:, :width] = jnp.zeros((3, width) + win.shape[2:], BF16)

    @pl.when(jnp.logical_not(has_next))
    def _():
        win[:, 2 * width :] = jnp.zeros((3, width) + win.shape[2:], BF16)

    @pl.when(jnp.logical_not(far_in))
    def _():
        win[far] = jnp.zeros(win.shape[1:], BF16)

    loads[0].wait()
    loads[-1].wait()
    for e in range(width):
        own = raw[e]
        win[1, width + e] = jnp.where(e < counts[0], own, jnp.zeros_like(own))

    total = 1 + half - 1
    for cond in (has_next, has_prev, far_out, far_in, far_in):
        total = total + cond.astype(jnp.int32)
    pl.semaphore_wait(barrier, total)

    direct = chunks[-1:]
    for k, j in chunks:
        if (k, j) in direct:
            pl.when(far_in)(lambda: s_copy(2, k, j).start())
        s_copy(0, k, j).start()
        for way in range(2):
            pl.when(e_out[way])(lambda: e_copy(way, 0, k, j).start())

    for load in loads[1:-1]:
        load.wait()
    values = (jnp.int32(0), 1 - 2 * side, 2 * side - 1)
    picks = []
    for value in values:
        pick = jnp.int32(nbr - 1)
        for n in range(nbr - 2, -1, -1):
            pick = jnp.where(neighbour[0, n] == value, n, pick)
        picks.append(pick)
    extra = nbr * (nbr - 1) // 2 - picks[0] - picks[1] - picks[2]
    picks.append(extra)
    extra_to = neighbour[0, extra]
    weights = []
    for i, pick in enumerate(picks):
        up, down = [None], [None]
        for d in range(1, width + 1):
            a = b = jnp.float32(0)
            for m in range(noff):
                hit = offsets[m] == d
                a = a + jnp.where(hit, phonon[0, m, 0, pick], 0.0)
                b = b + jnp.where(hit, phonon[0, m, 1, pick], 0.0)
            up.append(a)
            down.append(b)
        weights.append((up, down))
        re, im = coup[pick, 0], coup[pick, 1]
        coup_a[i, :size, :size] = re
        coup_a[i, :size, size:] = -im
        coup_a[i, size:, :size] = im
        coup_a[i, size:, size:] = re
        at = 2 * i * size
        coup_b[:size, at : at + size] = re
        coup_b[:size, at + size : at + 2 * size] = im
        coup_b[size:, at : at + size] = -im
        coup_b[size:, at + size : at + 2 * size] = re

    def pass_near(k, j):
        s_copy(0, k, j).wait_recv()
        if (k, j) not in direct:
            pl.when(far_out)(lambda: s_copy(1, k, j).start())
        for way in range(2):
            pl.when(e_out[way])(lambda: e_copy(way, 1, k, j).start())

    def pass_far(k, j):
        @pl.when(far_in)
        def _():
            s_copy(1, k, j).wait_recv()
            for way in range(2):
                pl.when(e_out[way])(lambda: e_copy(way, 2, k, j).start())

    def pair(e, p):
        return jnp.concatenate([win[1, e, p], win[1, e, p + 1]], axis=1)

    to_sibling = pltpu.make_async_remote_copy(
        src_ref=pair_tx,
        dst_ref=pair_rx,
        send_sem=pair_sem.at[0],
        recv_sem=pair_sem.at[1],
        device_id={"energy": sibling},
        device_id_type=mesh_type,
    )

    def own_polar():
        total = None
        for e in range(width):
            lower = jnp.concatenate(
                [pair(width + e + d, 0) for d in range(1, width + 1)], axis=0
            )
            re, im = win[1, width + e, 2], win[1, width + e, 3]
            upper = jnp.concatenate(
                [
                    jnp.concatenate([re, im], axis=1),
                    jnp.concatenate([-im, re], axis=1),
                ],
                axis=0,
            )
            term = lax.dot_general(lower, upper, NT, preferred_element_type=F32)
            total = term if total is None else total + term
        for m in range(noff):
            chosen = total[:size]
            for d in range(2, width + 1):
                chosen = jnp.where(
                    offsets[m] == d, total[(d - 1) * size : d * size], chosen
                )
            pol[2 * m * size : (2 * m + 1) * size] = chosen[:, :size]
            pol[(2 * m + 1) * size : (2 * m + 2) * size] = chosen[:, size:]
        padded = slabs.shape[1]
        for d in range(ne):
            if padded > rows:
                slabs[d, rows:] = jnp.zeros((padded - rows, size), F32)
            slabs[d, :rows] = pol[d * rows : (d + 1) * rows]

        def fill(q, carry):
            pair_tx[q] = slabs[2 * q + 1 - core].astype(BF16)
            return carry

        lax.fori_loop(0, half, fill, 0)
        to_sibling.start()

    def part_copy(k):
        there = lax.rem(chip + k, half)
        return pltpu.make_async_remote_copy(
            src_ref=part_tx.at[there],
            dst_ref=part_rx.at[chip],
            send_sem=part_send.at[k],
            recv_sem=part_recv.at[k],
            device_id={"energy": there * 2 + core},
            device_id_type=mesh_type,
        )

    def send_part(k, carry):
        there = lax.rem(chip + k, half)
        value = slabs[2 * there + core] + pair_rx[there].astype(F32)
        part_tx[there] = value.astype(BF16)
        part_copy(k).start()
        return carry

    tile = 16

    def halo(kind, k):
        for way in range(2):
            cond = e_in[way]
            if kind == 2:
                cond = jnp.logical_and(cond, far_in)
            pl.when(cond)(lambda: e_move(way, kind, 0, width, k, 1).wait_recv())

    def job(i, k):
        up, down = weights[i] if k == 0 else weights[i][::-1]
        for ri in range(2):
            p = 2 * k + ri

            def mix(t, carry, p=p, ri=ri):
                r = pl.multiple_of(t * tile, tile)

                def at_slot(slot):
                    return [
                        win[slot, e, p, pl.ds(r, tile), :] for e in range(3 * width)
                    ]

                if i < 3:
                    chosen = at_slot(slots[i])
                else:
                    g = [at_slot(c) for c in range(3)]
                    chosen = [
                        jnp.where(
                            extra_to == 0,
                            g[1][e],
                            jnp.where(extra_to < 0, g[0][e], g[2][e]),
                        )
                        for e in range(3 * width)
                    ]
                chosen = [c.astype(F32) for c in chosen]
                for e in range(width):
                    acc = None
                    for d in range(1, width + 1):
                        term = (
                            up[d] * chosen[width + e + d]
                            + down[d] * chosen[width + e - d]
                        )
                        acc = term if acc is None else acc + term
                    at = (k * width + e) * size
                    mixed[i, pl.ds(ri * size + r, tile), at : at + size] = acc.astype(
                        BF16
                    )
                return carry

            lax.fori_loop(0, size // tile, mix, 0)

        first = k * width * size
        y = lax.dot_general(
            coup_a[i],
            mixed[i, :, first : first + width * size],
            NN,
            preferred_element_type=F32,
        ).astype(BF16)
        for e in range(width):
            for ri in range(2):
                at = (2 * i + ri) * size
                left[first + e * size : first + (e + 1) * size, at : at + size] = y[
                    ri * size : (ri + 1) * size, e * size : (e + 1) * size
                ]

    def finish(k):
        first = k * width * size
        out = lax.dot_general(
            left[first : first + width * size],
            coup_b[...],
            NT,
            preferred_element_type=F32,
        )
        for e in range(width):
            for ri in range(2):
                sigma[e, 0, 2 * k + ri] = out[
                    e * size : (e + 1) * size, ri * size : (ri + 1) * size
                ]
        stores[k].start()

    def wait_part(k, carry):
        part_copy(k).wait()
        return carry

    def add_part(k, acc):
        return acc + part_rx[lax.rem(chip + k, half)].astype(F32)

    last = len(chunks) - 1
    for i in range(2):
        pass_near(*chunks[i])
    halo(0, 0)
    own_polar()
    for i in range(2, last):
        pass_near(*chunks[i])
        pass_far(*chunks[i - 2])
    job(0, 0)
    pass_far(*chunks[last])
    pass_near(*chunks[last])
    pass_far(*chunks[last - 2])
    to_sibling.wait_recv()
    lax.fori_loop(1, half, send_part, 0)
    halo(0, 1)
    job(0, 1)
    pass_far(*chunks[last - 1])
    halo(1, 0)
    job(1, 0)
    halo(1, 1)
    job(1, 1)
    halo(2, 0)
    job(2, 0)
    job(3, 0)
    finish(0)
    lax.fori_loop(1, half, wait_part, 0)
    mine = slabs[me] + pair_rx[chip].astype(F32)
    mine = lax.fori_loop(1, half, add_part, mine)
    polar[0] = mine[:rows]
    stores[2].start()
    halo(2, 1)
    job(2, 1)
    job(3, 1)
    finish(1)

    to_sibling.wait_send()
    for k, j in chunks:
        s_copy(0, k, j).wait_send()
        if (k, j) in direct:
            pl.when(far_in)(lambda: s_copy(2, k, j).wait_send())
        else:
            pl.when(far_out)(lambda: s_copy(1, k, j).wait_send())
    for way in range(2):
        for kind in range(3):
            cond = e_out[way]
            if kind == 2:
                cond = jnp.logical_and(cond, far_in)
            pl.when(cond)(lambda: e_move(way, kind, 0, width, 0, 2).wait_send())
    for store in stores:
        store.wait()


def deliver(sigma_in, polar_in, sigma, polar, sigma_at, polar_at, sems):
    width = sigma.shape[0]
    pieces = [
        (
            sigma_in.at[e, :, pl.ds(2 * k, 2)],
            sigma_at.at[e, :, pl.ds(2 * k, 2)],
            sigma.at[e, :, pl.ds(2 * k, 2)],
        )
        for k in range(2)
        for e in range(width)
    ]
    pieces.append((polar_in, polar_at, polar))
    ins = [
        pltpu.make_async_copy(a, b, sems.at[0, i]) for i, (a, b, _) in enumerate(pieces)
    ]
    outs = [
        pltpu.make_async_copy(b, c, sems.at[1, i]) for i, (_, b, c) in enumerate(pieces)
    ]
    for move in ins:
        move.start()
    for move, onward in zip(ins, outs):
        move.wait()
        onward.start()
    for onward in outs:
        onward.wait()


def local(ne, ns, green, couple, phonon, neighbour, offsets, counts):
    width, size = green.shape[0], green.shape[-1]
    nbr, noff = couple.shape[1], phonon.shape[2]
    rows = 2 * noff * size // ne
    padded = -(-rows // 16) * 16
    half = ne // 2
    hbm = pl.BlockSpec(memory_space=pltpu.HBM)
    dma = pltpu.SemaphoreType.DMA
    results = (
        jax.ShapeDtypeStruct(green.shape, F32),
        jax.ShapeDtypeStruct((1, rows, size), F32),
    )
    phonon = jnp.transpose(phonon, (0, 2, 3, 1))
    found = pl.pallas_call(
        functools.partial(kernel, ne, ns),
        out_shape=results,
        in_specs=[hbm] * 6,
        out_specs=(hbm, hbm),
        scratch_shapes=[
            pltpu.SMEM(phonon.shape, F32),
            pltpu.SMEM(neighbour.shape, jnp.int32),
            pltpu.SMEM(offsets.shape, jnp.int32),
            pltpu.SMEM(counts.shape, jnp.int32),
            pltpu.VMEM(green.shape, F32),
            pltpu.VMEM((1, rows, size), F32),
            pltpu.VMEM((width, 4, size, size), BF16),
            pltpu.VMEM((nbr, 2, size, size), BF16),
            pltpu.VMEM((3, 3 * width, 4, size, size), BF16),
            pltpu.VMEM((nbr, 2 * size, 2 * width * size), BF16),
            pltpu.VMEM((2 * width * size, 2 * nbr * size), BF16),
            pltpu.VMEM((nbr, 2 * size, 2 * size), BF16),
            pltpu.VMEM((2 * size, 2 * nbr * size), BF16),
            pltpu.VMEM((2 * noff * size, size), F32),
            pltpu.VMEM((ne, padded, size), F32),
            pltpu.VMEM((half, padded, size), BF16),
            pltpu.VMEM((half, padded, size), BF16),
            pltpu.VMEM((half, padded, size), BF16),
            pltpu.VMEM((half, padded, size), BF16),
            dma((6,)),
            dma((2, 3)),
            dma((2, 3, 2)),
            dma((3, 2, width)),
            dma((2, 2, width)),
            dma((2,)),
            dma((half,)),
            dma((half,)),
            dma((3,)),
        ],
        compiler_params=pltpu.CompilerParams(
            collective_id=0, has_side_effects=True, vmem_limit_bytes=60 * 1024 * 1024
        ),
        cost_estimate=pl.CostEstimate(
            flops=600_000_000, bytes_accessed=4_000_000, transcendentals=0
        ),
    )(phonon, neighbour, offsets, counts, green, couple)
    return pl.pallas_call(
        deliver,
        out_shape=results,
        in_specs=[hbm] * 2,
        out_specs=(hbm, hbm),
        scratch_shapes=[
            pltpu.VMEM(green.shape, F32),
            pltpu.VMEM((1, rows, size), F32),
            dma((2, 2 * width + 1)),
        ],
        compiler_params=pltpu.CompilerParams(vmem_limit_bytes=60 * 1024 * 1024),
    )(*found)


def solution(mesh):
    placed = (
        P("energy", "seg", None, None, None),
        P("seg", None, None, None, None),
        P("seg", None, None, None),
        P("seg", None),
        P(),
        P("energy"),
    )
    return jax.shard_map(
        functools.partial(local, mesh.shape["energy"], mesh.shape["seg"]),
        mesh=mesh,
        in_specs=placed,
        out_specs=(P("energy", "seg", None, None, None), P("seg", "energy", None)),
        check_vma=False,
    )
```

```python
import functools

import jax
import jax.numpy as jnp
from jax import lax
from jax.experimental import pallas as pl
from jax.experimental.pallas import tpu as pltpu
from jax.sharding import PartitionSpec as P

F32 = jnp.float32
BF16 = jnp.bfloat16
NT = (((1,), (1,)), ((), ()))
NN = (((1,), (0,)), ((), ()))


def kernel(
    ne,
    ns,
    phonon_in,
    neighbour_in,
    offsets_in,
    counts_in,
    green,
    couple,
    sigma_out,
    polar_out,
    phonon,
    neighbour,
    offsets,
    counts,
    sigma,
    polar,
    raw,
    coup,
    win,
    mixed,
    left,
    coup_a,
    coup_b,
    pol,
    slabs,
    pair_tx,
    pair_rx,
    part_tx,
    part_rx,
    load_sem,
    e_send,
    e_recv,
    s_send,
    s_recv,
    pair_sem,
    part_send,
    part_recv,
    out_sem,
):
    width, size = green.shape[0], green.shape[-1]
    nbr, noff = couple.shape[1], phonon_in.shape[1]
    rows = polar.shape[1]
    half = ne // 2
    me, seg = lax.axis_index("energy"), lax.axis_index("seg")
    core, chip = lax.rem(me, 2), lax.div(me, 2)
    sibling = me + 1 - 2 * core
    side = lax.rem(seg, 2)
    has_next, has_prev = me < ne - 1, me > 0
    partner = seg + 1 - 2 * side
    above, below = seg + 2 < ns, seg >= 2
    even = side == 0
    far_out = jnp.logical_or(
        jnp.logical_and(even, above), jnp.logical_and(jnp.logical_not(even), below)
    )
    far_in = jnp.logical_or(
        jnp.logical_and(even, below), jnp.logical_and(jnp.logical_not(even), above)
    )
    far_to = jnp.clip(seg + 2 - 4 * side, 0, ns - 1)
    far_from = jnp.clip(seg - 2 + 4 * side, 0, ns - 1)
    near, far = 2 - 2 * side, 2 * side
    slots = (1, near, far)
    mesh_type = pl.DeviceIdType.MESH
    chunks = [(k, j) for k in range(2) for j in range(width)]

    loads = [
        pltpu.make_async_copy(green.at[:, 0], raw, load_sem.at[0]),
        pltpu.make_async_copy(couple.at[0], coup, load_sem.at[1]),
        pltpu.make_async_copy(phonon_in, phonon, load_sem.at[2]),
        pltpu.make_async_copy(neighbour_in, neighbour, load_sem.at[3]),
        pltpu.make_async_copy(offsets_in, offsets, load_sem.at[4]),
        pltpu.make_async_copy(counts_in, counts, load_sem.at[5]),
    ]
    stores = [
        pltpu.make_async_copy(
            sigma.at[:, :, pl.ds(2 * k, 2)],
            sigma_out.at[:, :, pl.ds(2 * k, 2)],
            out_sem.at[k],
        )
        for k in range(2)
    ]
    stores.append(pltpu.make_async_copy(polar, polar_out, out_sem.at[2]))

    def e_move(way, kind, first, count, k, kinds):
        there = jnp.minimum(me + 1, ne - 1) if way == 0 else jnp.maximum(me - 1, 0)
        parts = pl.ds(2 * k, 2 * kinds)
        return pltpu.make_async_remote_copy(
            src_ref=win.at[slots[kind], pl.ds(width + first, count), parts],
            dst_ref=win.at[slots[kind], pl.ds(2 * width * way + first, count), parts],
            send_sem=e_send.at[way, kind],
            recv_sem=e_recv.at[way, kind, k],
            device_id={"energy": there},
            device_id_type=mesh_type,
        )

    def e_copy(way, kind, k, j):
        return e_move(way, kind, j, 1, k, 1)

    def s_copy(kind, k, j):
        return pltpu.make_async_remote_copy(
            src_ref=win.at[near if kind else 1, width + j, pl.ds(2 * k, 2)],
            dst_ref=win.at[far, width + j, pl.ds(2 * k, 2)],
            send_sem=s_send.at[kind, k, j],
            recv_sem=s_recv.at[kind, k, j],
            device_id={"seg": (partner, far_to)[kind]},
            device_id_type=mesh_type,
        )

    e_out, e_in = (has_next, has_prev), (has_prev, has_next)

    barrier = pltpu.get_barrier_semaphore()

    def greet(where):
        pl.semaphore_signal(barrier, inc=1, device_id=where, device_id_type=mesh_type)

    pl.when(has_next)(lambda: greet({"energy": jnp.minimum(me + 1, ne - 1)}))
    pl.when(has_prev)(lambda: greet({"energy": jnp.maximum(me - 1, 0)}))
    greet({"seg": partner})
    pl.when(far_out)(lambda: greet({"seg": far_to}))
    pl.when(far_in)(lambda: greet({"seg": far_from}))

    def greet_part(k, carry):
        greet({"energy": lax.rem(chip + k, half) * 2 + core})
        return carry

    lax.fori_loop(1, half, greet_part, 0)
    for load in loads:
        load.start()

    @pl.when(jnp.logical_not(has_prev))
    def _():
        win[:, :width] = jnp.zeros((3, width) + win.shape[2:], BF16)

    @pl.when(jnp.logical_not(has_next))
    def _():
        win[:, 2 * width :] = jnp.zeros((3, width) + win.shape[2:], BF16)

    @pl.when(jnp.logical_not(far_in))
    def _():
        win[far] = jnp.zeros(win.shape[1:], BF16)

    loads[0].wait()
    loads[-1].wait()
    for e in range(width):
        own = raw[e]
        win[1, width + e] = jnp.where(e < counts[0], own, jnp.zeros_like(own))

    total = 1 + half - 1
    for cond in (has_next, has_prev, far_out, far_in):
        total = total + cond.astype(jnp.int32)
    pl.semaphore_wait(barrier, total)

    for k, j in chunks:
        s_copy(0, k, j).start()
    for k, j in chunks:
        for way in range(2):
            pl.when(e_out[way])(lambda: e_copy(way, 0, k, j).start())

    for load in loads[1:-1]:
        load.wait()
    values = (jnp.int32(0), 1 - 2 * side, 2 * side - 1)
    picks = []
    for value in values:
        pick = jnp.int32(nbr - 1)
        for n in range(nbr - 2, -1, -1):
            pick = jnp.where(neighbour[0, n] == value, n, pick)
        picks.append(pick)
    extra = nbr * (nbr - 1) // 2 - picks[0] - picks[1] - picks[2]
    picks.append(extra)
    extra_to = neighbour[0, extra]
    weights = []
    for i, pick in enumerate(picks):
        up, down = [None], [None]
        for d in range(1, width + 1):
            a = b = jnp.float32(0)
            for m in range(noff):
                hit = offsets[m] == d
                a = a + jnp.where(hit, phonon[0, m, 0, pick], 0.0)
                b = b + jnp.where(hit, phonon[0, m, 1, pick], 0.0)
            up.append(a)
            down.append(b)
        weights.append((up, down))
        re, im = coup[pick, 0], coup[pick, 1]
        coup_a[i, :size, :size] = re
        coup_a[i, :size, size:] = -im
        coup_a[i, size:, :size] = im
        coup_a[i, size:, size:] = re
        at = 2 * i * size
        coup_b[:size, at : at + size] = re
        coup_b[:size, at + size : at + 2 * size] = im
        coup_b[size:, at : at + size] = -im
        coup_b[size:, at + size : at + 2 * size] = re

    def pass_near(k, j):
        s_copy(0, k, j).wait_recv()
        pl.when(far_out)(lambda: s_copy(1, k, j).start())
        for way in range(2):
            pl.when(e_out[way])(lambda: e_copy(way, 1, k, j).start())

    def pass_far(k, j):
        @pl.when(far_in)
        def _():
            s_copy(1, k, j).wait_recv()
            for way in range(2):
                pl.when(e_out[way])(lambda: e_copy(way, 2, k, j).start())

    def pair(e, p):
        return jnp.concatenate([win[1, e, p], win[1, e, p + 1]], axis=1)

    to_sibling = pltpu.make_async_remote_copy(
        src_ref=pair_tx,
        dst_ref=pair_rx,
        send_sem=pair_sem.at[0],
        recv_sem=pair_sem.at[1],
        device_id={"energy": sibling},
        device_id_type=mesh_type,
    )

    def own_polar():
        total = None
        for e in range(width):
            lower = jnp.concatenate(
                [pair(width + e + d, 0) for d in range(1, width + 1)], axis=0
            )
            re, im = win[1, width + e, 2], win[1, width + e, 3]
            upper = jnp.concatenate(
                [
                    jnp.concatenate([re, im], axis=1),
                    jnp.concatenate([-im, re], axis=1),
                ],
                axis=0,
            )
            term = lax.dot_general(lower, upper, NT, preferred_element_type=F32)
            total = term if total is None else total + term
        for m in range(noff):
            chosen = total[:size]
            for d in range(2, width + 1):
                chosen = jnp.where(
                    offsets[m] == d, total[(d - 1) * size : d * size], chosen
                )
            pol[2 * m * size : (2 * m + 1) * size] = chosen[:, :size]
            pol[(2 * m + 1) * size : (2 * m + 2) * size] = chosen[:, size:]
        padded = slabs.shape[1]
        for d in range(ne):
            if padded > rows:
                slabs[d, rows:] = jnp.zeros((padded - rows, size), F32)
            slabs[d, :rows] = pol[d * rows : (d + 1) * rows]

        def fill(q, carry):
            pair_tx[q] = slabs[2 * q + 1 - core].astype(BF16)
            return carry

        lax.fori_loop(0, half, fill, 0)
        to_sibling.start()

    def part_copy(k):
        there = lax.rem(chip + k, half)
        return pltpu.make_async_remote_copy(
            src_ref=part_tx.at[there],
            dst_ref=part_rx.at[chip],
            send_sem=part_send.at[k],
            recv_sem=part_recv.at[k],
            device_id={"energy": there * 2 + core},
            device_id_type=mesh_type,
        )

    def send_part(k, carry):
        there = lax.rem(chip + k, half)
        value = slabs[2 * there + core] + pair_rx[there].astype(F32)
        part_tx[there] = value.astype(BF16)
        part_copy(k).start()
        return carry

    tile = 16

    def halo(kind, k):
        for way in range(2):
            cond = e_in[way]
            if kind == 2:
                cond = jnp.logical_and(cond, far_in)
            pl.when(cond)(lambda: e_move(way, kind, 0, width, k, 1).wait_recv())

    def job(i, k):
        up, down = weights[i] if k == 0 else weights[i][::-1]
        for ri in range(2):
            p = 2 * k + ri

            def mix(t, carry, p=p, ri=ri):
                r = pl.multiple_of(t * tile, tile)

                def at_slot(slot):
                    return [
                        win[slot, e, p, pl.ds(r, tile), :] for e in range(3 * width)
                    ]

                if i < 3:
                    chosen = at_slot(slots[i])
                else:
                    g = [at_slot(c) for c in range(3)]
                    chosen = [
                        jnp.where(
                            extra_to == 0,
                            g[1][e],
                            jnp.where(extra_to < 0, g[0][e], g[2][e]),
                        )
                        for e in range(3 * width)
                    ]
                chosen = [c.astype(F32) for c in chosen]
                for e in range(width):
                    acc = None
                    for d in range(1, width + 1):
                        term = (
                            up[d] * chosen[width + e + d]
                            + down[d] * chosen[width + e - d]
                        )
                        acc = term if acc is None else acc + term
                    at = (k * width + e) * size
                    mixed[i, pl.ds(ri * size + r, tile), at : at + size] = acc.astype(
                        BF16
                    )
                return carry

            lax.fori_loop(0, size // tile, mix, 0)

        first = k * width * size
        y = lax.dot_general(
            coup_a[i],
            mixed[i, :, first : first + width * size],
            NN,
            preferred_element_type=F32,
        ).astype(BF16)
        for e in range(width):
            for ri in range(2):
                at = (2 * i + ri) * size
                left[first + e * size : first + (e + 1) * size, at : at + size] = y[
                    ri * size : (ri + 1) * size, e * size : (e + 1) * size
                ]

    def finish(k):
        first = k * width * size
        out = lax.dot_general(
            left[first : first + width * size],
            coup_b[...],
            NT,
            preferred_element_type=F32,
        )
        for e in range(width):
            for ri in range(2):
                sigma[e, 0, 2 * k + ri] = out[
                    e * size : (e + 1) * size, ri * size : (ri + 1) * size
                ]
        stores[k].start()

    def wait_part(k, carry):
        part_copy(k).wait()
        return carry

    def add_part(k, acc):
        return acc + part_rx[lax.rem(chip + k, half)].astype(F32)

    last = len(chunks) - 1
    for i in range(last):
        pass_near(*chunks[i])
        if i >= 2:
            pass_far(*chunks[i - 2])
    halo(0, 0)
    own_polar()
    pass_near(*chunks[last])
    pass_far(*chunks[last - 2])
    job(0, 0)
    pass_far(*chunks[last - 1])
    to_sibling.wait_recv()
    lax.fori_loop(1, half, send_part, 0)
    pass_far(*chunks[last])
    halo(0, 1)
    job(0, 1)
    halo(1, 0)
    job(1, 0)
    halo(1, 1)
    job(1, 1)
    halo(2, 0)
    job(2, 0)
    job(3, 0)
    finish(0)
    lax.fori_loop(1, half, wait_part, 0)
    mine = slabs[me] + pair_rx[chip].astype(F32)
    mine = lax.fori_loop(1, half, add_part, mine)
    polar[0] = mine[:rows]
    stores[2].start()
    halo(2, 1)
    job(2, 1)
    job(3, 1)
    finish(1)

    to_sibling.wait_send()
    for k, j in chunks:
        s_copy(0, k, j).wait_send()
        pl.when(far_out)(lambda: s_copy(1, k, j).wait_send())
    for way in range(2):
        for kind in range(3):
            cond = e_out[way]
            if kind == 2:
                cond = jnp.logical_and(cond, far_in)
            pl.when(cond)(lambda: e_move(way, kind, 0, width, 0, 2).wait_send())
    for store in stores:
        store.wait()


def deliver(sigma_in, polar_in, sigma, polar, sigma_at, polar_at, sems):
    width = sigma.shape[0]
    pieces = [
        (
            sigma_in.at[e, :, pl.ds(2 * k, 2)],
            sigma_at.at[e, :, pl.ds(2 * k, 2)],
            sigma.at[e, :, pl.ds(2 * k, 2)],
        )
        for k in range(2)
        for e in range(width)
    ]
    pieces.append((polar_in, polar_at, polar))
    ins = [
        pltpu.make_async_copy(a, b, sems.at[0, i]) for i, (a, b, _) in enumerate(pieces)
    ]
    outs = [
        pltpu.make_async_copy(b, c, sems.at[1, i]) for i, (_, b, c) in enumerate(pieces)
    ]
    for move in ins:
        move.start()
    for move, onward in zip(ins, outs):
        move.wait()
        onward.start()
    for onward in outs:
        onward.wait()


def local(ne, ns, green, couple, phonon, neighbour, offsets, counts):
    width, size = green.shape[0], green.shape[-1]
    nbr, noff = couple.shape[1], phonon.shape[2]
    rows = 2 * noff * size // ne
    padded = -(-rows // 16) * 16
    half = ne // 2
    hbm = pl.BlockSpec(memory_space=pltpu.HBM)
    dma = pltpu.SemaphoreType.DMA
    results = (
        jax.ShapeDtypeStruct(green.shape, F32),
        jax.ShapeDtypeStruct((1, rows, size), F32),
    )
    phonon = jnp.transpose(phonon, (0, 2, 3, 1))
    found = pl.pallas_call(
        functools.partial(kernel, ne, ns),
        out_shape=results,
        in_specs=[hbm] * 6,
        out_specs=(hbm, hbm),
        scratch_shapes=[
            pltpu.SMEM(phonon.shape, F32),
            pltpu.SMEM(neighbour.shape, jnp.int32),
            pltpu.SMEM(offsets.shape, jnp.int32),
            pltpu.SMEM(counts.shape, jnp.int32),
            pltpu.VMEM(green.shape, F32),
            pltpu.VMEM((1, rows, size), F32),
            pltpu.VMEM((width, 4, size, size), BF16),
            pltpu.VMEM((nbr, 2, size, size), BF16),
            pltpu.VMEM((3, 3 * width, 4, size, size), BF16),
            pltpu.VMEM((nbr, 2 * size, 2 * width * size), BF16),
            pltpu.VMEM((2 * width * size, 2 * nbr * size), BF16),
            pltpu.VMEM((nbr, 2 * size, 2 * size), BF16),
            pltpu.VMEM((2 * size, 2 * nbr * size), BF16),
            pltpu.VMEM((2 * noff * size, size), F32),
            pltpu.VMEM((ne, padded, size), F32),
            pltpu.VMEM((half, padded, size), BF16),
            pltpu.VMEM((half, padded, size), BF16),
            pltpu.VMEM((half, padded, size), BF16),
            pltpu.VMEM((half, padded, size), BF16),
            dma((6,)),
            dma((2, 3)),
            dma((2, 3, 2)),
            dma((2, 2, width)),
            dma((2, 2, width)),
            dma((2,)),
            dma((half,)),
            dma((half,)),
            dma((3,)),
        ],
        compiler_params=pltpu.CompilerParams(
            collective_id=0, has_side_effects=True, vmem_limit_bytes=60 * 1024 * 1024
        ),
        cost_estimate=pl.CostEstimate(
            flops=600_000_000, bytes_accessed=4_000_000, transcendentals=0
        ),
    )(phonon, neighbour, offsets, counts, green, couple)
    return pl.pallas_call(
        deliver,
        out_shape=results,
        in_specs=[hbm] * 2,
        out_specs=(hbm, hbm),
        scratch_shapes=[
            pltpu.VMEM(green.shape, F32),
            pltpu.VMEM((1, rows, size), F32),
            dma((2, 2 * width + 1)),
        ],
        compiler_params=pltpu.CompilerParams(vmem_limit_bytes=60 * 1024 * 1024),
    )(*found)


def solution(mesh):
    placed = (
        P("energy", "seg", None, None, None),
        P("seg", None, None, None, None),
        P("seg", None, None, None),
        P("seg", None),
        P(),
        P("energy"),
    )
    return jax.shard_map(
        functools.partial(local, mesh.shape["energy"], mesh.shape["seg"]),
        mesh=mesh,
        in_specs=placed,
        out_specs=(P("energy", "seg", None, None, None), P("seg", "energy", None)),
        check_vma=False,
    )
```

```python
import functools

import jax
import jax.numpy as jnp
from jax import lax
from jax.experimental import pallas as pl
from jax.experimental.pallas import tpu as pltpu
from jax.sharding import PartitionSpec as P

F32 = jnp.float32
BF16 = jnp.bfloat16
NT = (((1,), (1,)), ((), ()))
NN = (((1,), (0,)), ((), ()))


def kernel(
    ne,
    ns,
    phonon_in,
    neighbour_in,
    offsets_in,
    counts_in,
    green,
    couple,
    sigma_out,
    polar_out,
    phonon,
    neighbour,
    offsets,
    counts,
    sigma,
    polar,
    raw,
    coup,
    win,
    mixed,
    left,
    coup_a,
    coup_b,
    pol,
    slabs,
    pair_tx,
    pair_rx,
    part_tx,
    part_rx,
    load_sem,
    e_send,
    e_recv,
    s_send,
    s_recv,
    pair_sem,
    part_send,
    part_recv,
    out_sem,
    corner_sem,
):
    width, size = green.shape[0], green.shape[-1]
    nbr, noff = couple.shape[1], phonon_in.shape[1]
    rows = polar.shape[1]
    half = ne // 2
    me, seg = lax.axis_index("energy"), lax.axis_index("seg")
    core, chip = lax.rem(me, 2), lax.div(me, 2)
    sibling = me + 1 - 2 * core
    side = lax.rem(seg, 2)
    has_next, has_prev = me < ne - 1, me > 0
    partner = seg + 1 - 2 * side
    above, below = seg + 2 < ns, seg >= 2
    even = side == 0
    far_out = jnp.logical_or(
        jnp.logical_and(even, above), jnp.logical_and(jnp.logical_not(even), below)
    )
    far_in = jnp.logical_or(
        jnp.logical_and(even, below), jnp.logical_and(jnp.logical_not(even), above)
    )
    far_to = jnp.clip(seg + 2 - 4 * side, 0, ns - 1)
    far_from = jnp.clip(seg - 2 + 4 * side, 0, ns - 1)
    near, far = 2 - 2 * side, 2 * side
    slots = (1, near, far)
    mesh_type = pl.DeviceIdType.MESH
    chunks = [(k, j) for k in range(2) for j in range(width)]

    loads = [
        pltpu.make_async_copy(green.at[:, 0], raw, load_sem.at[0]),
        pltpu.make_async_copy(couple.at[0], coup, load_sem.at[1]),
        pltpu.make_async_copy(phonon_in, phonon, load_sem.at[2]),
        pltpu.make_async_copy(neighbour_in, neighbour, load_sem.at[3]),
        pltpu.make_async_copy(offsets_in, offsets, load_sem.at[4]),
        pltpu.make_async_copy(counts_in, counts, load_sem.at[5]),
    ]
    stores = [
        pltpu.make_async_copy(
            sigma.at[:, :, pl.ds(2 * k, 2)],
            sigma_out.at[:, :, pl.ds(2 * k, 2)],
            out_sem.at[k],
        )
        for k in range(2)
    ]
    stores.append(pltpu.make_async_copy(polar, polar_out, out_sem.at[2]))

    def e_move(way, kind, first, count, k, kinds):
        there = jnp.minimum(me + 1, ne - 1) if way == 0 else jnp.maximum(me - 1, 0)
        parts = pl.ds(2 * k, 2 * kinds)
        return pltpu.make_async_remote_copy(
            src_ref=win.at[slots[kind], pl.ds(width + first, count), parts],
            dst_ref=win.at[slots[kind], pl.ds(2 * width * way + first, count), parts],
            send_sem=e_send.at[way, kind],
            recv_sem=e_recv.at[way, kind, k],
            device_id={"energy": there},
            device_id_type=mesh_type,
        )

    def e_copy(way, kind, k, j):
        return e_move(way, kind, j, 1, k, 1)

    def s_copy(kind, k, j):
        return pltpu.make_async_remote_copy(
            src_ref=win.at[near if kind else 1, width + j, pl.ds(2 * k, 2)],
            dst_ref=win.at[far, width + j, pl.ds(2 * k, 2)],
            send_sem=s_send.at[kind, k, j],
            recv_sem=s_recv.at[kind, k, j],
            device_id={"seg": (partner, far_to)[kind]},
            device_id_type=mesh_type,
        )

    e_out, e_in = (has_next, has_prev), (has_prev, has_next)
    edge_in = jnp.logical_or(
        jnp.logical_and(core == 0, has_prev), jnp.logical_and(core == 1, has_next)
    )

    def corner_copy():
        there = pl.ds(2 * width * core, width)
        return pltpu.make_async_remote_copy(
            src_ref=win.at[1, there, pl.ds(2, 2)],
            dst_ref=win.at[far, there, pl.ds(2, 2)],
            send_sem=corner_sem.at[0],
            recv_sem=corner_sem.at[1],
            device_id={"seg": partner},
            device_id_type=mesh_type,
        )

    barrier = pltpu.get_barrier_semaphore()

    def greet(where):
        pl.semaphore_signal(barrier, inc=1, device_id=where, device_id_type=mesh_type)

    pl.when(has_next)(lambda: greet({"energy": jnp.minimum(me + 1, ne - 1)}))
    pl.when(has_prev)(lambda: greet({"energy": jnp.maximum(me - 1, 0)}))
    greet({"seg": partner})
    pl.when(far_out)(lambda: greet({"seg": far_to}))
    pl.when(far_in)(lambda: greet({"seg": far_from}))

    def greet_part(k, carry):
        greet({"energy": lax.rem(chip + k, half) * 2 + core})
        return carry

    lax.fori_loop(1, half, greet_part, 0)
    for load in loads:
        load.start()

    @pl.when(jnp.logical_not(has_prev))
    def _():
        win[:, :width] = jnp.zeros((3, width) + win.shape[2:], BF16)

    @pl.when(jnp.logical_not(has_next))
    def _():
        win[:, 2 * width :] = jnp.zeros((3, width) + win.shape[2:], BF16)

    @pl.when(jnp.logical_not(far_in))
    def _():
        win[far] = jnp.zeros(win.shape[1:], BF16)

    loads[0].wait()
    loads[-1].wait()
    for e in range(width):
        own = raw[e]
        win[1, width + e] = jnp.where(e < counts[0], own, jnp.zeros_like(own))

    total = 1 + half - 1
    for cond in (has_next, has_prev, far_out, far_in):
        total = total + cond.astype(jnp.int32)
    pl.semaphore_wait(barrier, total)

    for k, j in chunks:
        s_copy(0, k, j).start()
    for k, j in chunks:
        for way in range(2):
            pl.when(e_out[way])(lambda: e_copy(way, 0, k, j).start())

    for load in loads[1:-1]:
        load.wait()
    values = (jnp.int32(0), 1 - 2 * side, 2 * side - 1)
    picks = []
    for value in values:
        pick = jnp.int32(nbr - 1)
        for n in range(nbr - 2, -1, -1):
            pick = jnp.where(neighbour[0, n] == value, n, pick)
        picks.append(pick)
    extra = nbr * (nbr - 1) // 2 - picks[0] - picks[1] - picks[2]
    picks.append(extra)
    extra_to = neighbour[0, extra]
    weights = []
    for i, pick in enumerate(picks):
        up, down = [None], [None]
        for d in range(1, width + 1):
            a = b = jnp.float32(0)
            for m in range(noff):
                hit = offsets[m] == d
                a = a + jnp.where(hit, phonon[0, m, 0, pick], 0.0)
                b = b + jnp.where(hit, phonon[0, m, 1, pick], 0.0)
            up.append(a)
            down.append(b)
        weights.append((up, down))
        re, im = coup[pick, 0], coup[pick, 1]
        coup_a[i, :size, :size] = re
        coup_a[i, :size, size:] = -im
        coup_a[i, size:, :size] = im
        coup_a[i, size:, size:] = re
        at = 2 * i * size
        coup_b[:size, at : at + size] = re
        coup_b[:size, at + size : at + 2 * size] = im
        coup_b[size:, at : at + size] = -im
        coup_b[size:, at + size : at + 2 * size] = re

    def pass_near(k, j):
        s_copy(0, k, j).wait_recv()
        pl.when(far_out)(lambda: s_copy(1, k, j).start())
        for way in range(2):
            cond = e_out[way]
            if k == 1:
                cond = jnp.logical_and(cond, core == way)
            pl.when(cond)(lambda: e_copy(way, 1, k, j).start())

    def pass_far(k, j):
        @pl.when(far_in)
        def _():
            s_copy(1, k, j).wait_recv()
            for way in range(2):
                pl.when(e_out[way])(lambda: e_copy(way, 2, k, j).start())

    def pair(e, p):
        return jnp.concatenate([win[1, e, p], win[1, e, p + 1]], axis=1)

    to_sibling = pltpu.make_async_remote_copy(
        src_ref=pair_tx,
        dst_ref=pair_rx,
        send_sem=pair_sem.at[0],
        recv_sem=pair_sem.at[1],
        device_id={"energy": sibling},
        device_id_type=mesh_type,
    )

    def own_polar():
        total = None
        for e in range(width):
            lower = jnp.concatenate(
                [pair(width + e + d, 0) for d in range(1, width + 1)], axis=0
            )
            re, im = win[1, width + e, 2], win[1, width + e, 3]
            upper = jnp.concatenate(
                [
                    jnp.concatenate([re, im], axis=1),
                    jnp.concatenate([-im, re], axis=1),
                ],
                axis=0,
            )
            term = lax.dot_general(lower, upper, NT, preferred_element_type=F32)
            total = term if total is None else total + term
        for m in range(noff):
            chosen = total[:size]
            for d in range(2, width + 1):
                chosen = jnp.where(
                    offsets[m] == d, total[(d - 1) * size : d * size], chosen
                )
            pol[2 * m * size : (2 * m + 1) * size] = chosen[:, :size]
            pol[(2 * m + 1) * size : (2 * m + 2) * size] = chosen[:, size:]
        padded = slabs.shape[1]
        for d in range(ne):
            if padded > rows:
                slabs[d, rows:] = jnp.zeros((padded - rows, size), F32)
            slabs[d, :rows] = pol[d * rows : (d + 1) * rows]

        def fill(q, carry):
            pair_tx[q] = slabs[2 * q + 1 - core].astype(BF16)
            return carry

        lax.fori_loop(0, half, fill, 0)
        to_sibling.start()

    def part_copy(k):
        there = lax.rem(chip + k, half)
        return pltpu.make_async_remote_copy(
            src_ref=part_tx.at[there],
            dst_ref=part_rx.at[chip],
            send_sem=part_send.at[k],
            recv_sem=part_recv.at[k],
            device_id={"energy": there * 2 + core},
            device_id_type=mesh_type,
        )

    def send_part(k, carry):
        there = lax.rem(chip + k, half)
        value = slabs[2 * there + core] + pair_rx[there].astype(F32)
        part_tx[there] = value.astype(BF16)
        part_copy(k).start()
        return carry

    tile = 16

    def halo(kind, k):
        for way in range(2):
            cond = e_in[way]
            if kind == 2:
                cond = jnp.logical_and(cond, far_in)
            if (kind, k) == (1, 1):
                cond = jnp.logical_and(cond, core == 1 - way)
            pl.when(cond)(lambda: e_move(way, kind, 0, width, k, 1).wait_recv())
        if (kind, k) == (1, 1):
            pl.when(edge_in)(lambda: corner_copy().wait_recv())

    def job(i, k):
        up, down = weights[i] if k == 0 else weights[i][::-1]
        for ri in range(2):
            p = 2 * k + ri

            def mix(t, carry, p=p, ri=ri):
                r = pl.multiple_of(t * tile, tile)

                def at_slot(slot):
                    return [
                        win[slot, e, p, pl.ds(r, tile), :] for e in range(3 * width)
                    ]

                if i < 3:
                    chosen = at_slot(slots[i])
                else:
                    g = [at_slot(c) for c in range(3)]
                    chosen = [
                        jnp.where(
                            extra_to == 0,
                            g[1][e],
                            jnp.where(extra_to < 0, g[0][e], g[2][e]),
                        )
                        for e in range(3 * width)
                    ]
                chosen = [c.astype(F32) for c in chosen]
                for e in range(width):
                    acc = None
                    for d in range(1, width + 1):
                        term = (
                            up[d] * chosen[width + e + d]
                            + down[d] * chosen[width + e - d]
                        )
                        acc = term if acc is None else acc + term
                    at = (k * width + e) * size
                    mixed[i, pl.ds(ri * size + r, tile), at : at + size] = acc.astype(
                        BF16
                    )
                return carry

            lax.fori_loop(0, size // tile, mix, 0)

        first = k * width * size
        y = lax.dot_general(
            coup_a[i],
            mixed[i, :, first : first + width * size],
            NN,
            preferred_element_type=F32,
        ).astype(BF16)
        for e in range(width):
            for ri in range(2):
                at = (2 * i + ri) * size
                left[first + e * size : first + (e + 1) * size, at : at + size] = y[
                    ri * size : (ri + 1) * size, e * size : (e + 1) * size
                ]

    def finish(k):
        first = k * width * size
        out = lax.dot_general(
            left[first : first + width * size],
            coup_b[...],
            NT,
            preferred_element_type=F32,
        )
        for e in range(width):
            for ri in range(2):
                sigma[e, 0, 2 * k + ri] = out[
                    e * size : (e + 1) * size, ri * size : (ri + 1) * size
                ]
        stores[k].start()

    def wait_part(k, carry):
        part_copy(k).wait()
        return carry

    def add_part(k, acc):
        return acc + part_rx[lax.rem(chip + k, half)].astype(F32)

    last = len(chunks) - 1
    for i in range(last):
        pass_near(*chunks[i])
        if i >= 2:
            pass_far(*chunks[i - 2])
    halo(0, 0)
    own_polar()
    pass_near(*chunks[last])
    halo(0, 1)
    pl.when(edge_in)(lambda: corner_copy().start())
    pass_far(*chunks[last - 2])
    job(0, 0)
    pass_far(*chunks[last - 1])
    to_sibling.wait_recv()
    lax.fori_loop(1, half, send_part, 0)
    pass_far(*chunks[last])
    job(0, 1)
    halo(1, 0)
    job(1, 0)
    halo(1, 1)
    job(1, 1)
    halo(2, 0)
    job(2, 0)
    job(3, 0)
    finish(0)
    lax.fori_loop(1, half, wait_part, 0)
    mine = slabs[me] + pair_rx[chip].astype(F32)
    mine = lax.fori_loop(1, half, add_part, mine)
    polar[0] = mine[:rows]
    stores[2].start()
    halo(2, 1)
    job(2, 1)
    job(3, 1)
    finish(1)

    to_sibling.wait_send()
    for k, j in chunks:
        s_copy(0, k, j).wait_send()
        pl.when(far_out)(lambda: s_copy(1, k, j).wait_send())
    for way in range(2):
        for kind in range(3):
            cond = e_out[way]
            if kind == 2:
                cond = jnp.logical_and(cond, far_in)
            if kind == 1:
                part = jnp.logical_and(cond, core != way)
                pl.when(part)(lambda: e_move(way, kind, 0, width, 0, 1).wait_send())
                cond = jnp.logical_and(cond, core == way)
            pl.when(cond)(lambda: e_move(way, kind, 0, width, 0, 2).wait_send())
    pl.when(edge_in)(lambda: corner_copy().wait_send())
    for store in stores:
        store.wait()


def deliver(sigma_in, polar_in, sigma, polar, sigma_at, polar_at, sems):
    width = sigma.shape[0]
    pieces = [
        (
            sigma_in.at[e, :, pl.ds(2 * k, 2)],
            sigma_at.at[e, :, pl.ds(2 * k, 2)],
            sigma.at[e, :, pl.ds(2 * k, 2)],
        )
        for k in range(2)
        for e in range(width)
    ]
    pieces.append((polar_in, polar_at, polar))
    ins = [
        pltpu.make_async_copy(a, b, sems.at[0, i]) for i, (a, b, _) in enumerate(pieces)
    ]
    outs = [
        pltpu.make_async_copy(b, c, sems.at[1, i]) for i, (_, b, c) in enumerate(pieces)
    ]
    for move in ins:
        move.start()
    for move, onward in zip(ins, outs):
        move.wait()
        onward.start()
    for onward in outs:
        onward.wait()


def local(ne, ns, green, couple, phonon, neighbour, offsets, counts):
    width, size = green.shape[0], green.shape[-1]
    nbr, noff = couple.shape[1], phonon.shape[2]
    rows = 2 * noff * size // ne
    padded = -(-rows // 16) * 16
    half = ne // 2
    hbm = pl.BlockSpec(memory_space=pltpu.HBM)
    dma = pltpu.SemaphoreType.DMA
    results = (
        jax.ShapeDtypeStruct(green.shape, F32),
        jax.ShapeDtypeStruct((1, rows, size), F32),
    )
    phonon = jnp.transpose(phonon, (0, 2, 3, 1))
    found = pl.pallas_call(
        functools.partial(kernel, ne, ns),
        out_shape=results,
        in_specs=[hbm] * 6,
        out_specs=(hbm, hbm),
        scratch_shapes=[
            pltpu.SMEM(phonon.shape, F32),
            pltpu.SMEM(neighbour.shape, jnp.int32),
            pltpu.SMEM(offsets.shape, jnp.int32),
            pltpu.SMEM(counts.shape, jnp.int32),
            pltpu.VMEM(green.shape, F32),
            pltpu.VMEM((1, rows, size), F32),
            pltpu.VMEM((width, 4, size, size), BF16),
            pltpu.VMEM((nbr, 2, size, size), BF16),
            pltpu.VMEM((3, 3 * width, 4, size, size), BF16),
            pltpu.VMEM((nbr, 2 * size, 2 * width * size), BF16),
            pltpu.VMEM((2 * width * size, 2 * nbr * size), BF16),
            pltpu.VMEM((nbr, 2 * size, 2 * size), BF16),
            pltpu.VMEM((2 * size, 2 * nbr * size), BF16),
            pltpu.VMEM((2 * noff * size, size), F32),
            pltpu.VMEM((ne, padded, size), F32),
            pltpu.VMEM((half, padded, size), BF16),
            pltpu.VMEM((half, padded, size), BF16),
            pltpu.VMEM((half, padded, size), BF16),
            pltpu.VMEM((half, padded, size), BF16),
            dma((6,)),
            dma((2, 3)),
            dma((2, 3, 2)),
            dma((2, 2, width)),
            dma((2, 2, width)),
            dma((2,)),
            dma((half,)),
            dma((half,)),
            dma((3,)),
            dma((2,)),
        ],
        compiler_params=pltpu.CompilerParams(
            collective_id=0, has_side_effects=True, vmem_limit_bytes=60 * 1024 * 1024
        ),
        cost_estimate=pl.CostEstimate(
            flops=600_000_000, bytes_accessed=4_000_000, transcendentals=0
        ),
    )(phonon, neighbour, offsets, counts, green, couple)
    return pl.pallas_call(
        deliver,
        out_shape=results,
        in_specs=[hbm] * 2,
        out_specs=(hbm, hbm),
        scratch_shapes=[
            pltpu.VMEM(green.shape, F32),
            pltpu.VMEM((1, rows, size), F32),
            dma((2, 2 * width + 1)),
        ],
        compiler_params=pltpu.CompilerParams(vmem_limit_bytes=60 * 1024 * 1024),
    )(*found)


def solution(mesh):
    placed = (
        P("energy", "seg", None, None, None),
        P("seg", None, None, None, None),
        P("seg", None, None, None),
        P("seg", None),
        P(),
        P("energy"),
    )
    return jax.shard_map(
        functools.partial(local, mesh.shape["energy"], mesh.shape["seg"]),
        mesh=mesh,
        in_specs=placed,
        out_specs=(P("energy", "seg", None, None, None), P("seg", "energy", None)),
        check_vma=False,
    )
```
